256 devices in a mesh: dp: 128 (over y, z, x), tensor: 2 (over core).
Axes of the slice: x: 4, y: 4, z: 8, core: 2. Of those that a mesh axis runs over, the one named last changes fastest.
Arguments:
- layer_in: bfloat16 [98304, 1280], P('dp'), may hold values from -6 to 6
- ssm_in: bfloat16 [98304, 2560], P('dp', 'tensor'), may hold values from -6 to 6
- b_in: bfloat16 [98304, 128], P('dp'), may hold values from -1.5 to 1.5
- c_in: bfloat16 [98304, 128], P('dp'), may hold values from -1.5 to 1.5
- log_decay: float32 [98304, 40], P('dp', 'tensor'), may hold values from -1.5 to 0
- skip_gain: float32 [40], P('tensor'), may hold values from 0.5 to 1.5
- grad_out: bfloat16 [98304, 2560], P('dp', 'tensor'), may hold values from -6 to 6
- q_seed: int32 [1], replicated, may hold values from 0 to 46336
- error_in: bfloat16 [128, 1280, 2560], P('dp', None, 'tensor'), may hold values from -1.6 to 1.6
Outputs:
- grad_bc: float32 [98304, 256], P('dp')
- factor_p: float32 [64, 1280], P('tensor')
- factor_q: float32 [32, 2560], P(None, 'tensor')
- error_out: bfloat16 [128, 1280, 2560], P('dp', None, 'tensor')
The draws below stay inside these ranges and needn't reach their ends.
All inputs are finite; a program needn't handle non-finite values.
Results may differ from the reference program's by a relative error of at most 0.0034.
The reference program's roundings to bfloat16 on the way count: a program that leaves them out, or rounds other values in their place, can miss the bound.
Values sent between devices are 32-bit elements; how exact they have to be, the bound alone decides.
A program may use at most 128 MiB of HBM per device.

```python
import math
import jax
import jax.numpy as jnp
from jax import lax

D = 1280
HEAD_GROUP = 40
HEADDIM = 64
NSTATE = 128
SPAN = 256
R = 32
REPLICA_TOKENS = 768
E = 2560
TOKENS = 98304
REPLICAS = 128
RANKS = 64
N_DP = 128
N_TENSOR = 2


def draw_log_decay(key, part):
    key = jax.random.fold_in(key, 7)
    rate_key, wobble_key, replica_key, outburst_key, loss_key = jax.random.split(key, 5)
    head_groups = TOKENS // REPLICA_TOKENS
    lowest_rate = 0.3 / REPLICA_TOKENS
    highest_rate = 1.0 / 30.0
    spread = jax.random.uniform(rate_key, (HEAD_GROUP,), jnp.float32)
    per_head_rates = jnp.exp(jnp.log(lowest_rate) + spread * (jnp.log(highest_rate) - jnp.log(lowest_rate)))
    random_wobble = jax.random.uniform(wobble_key, (head_groups, REPLICA_TOKENS, HEAD_GROUP), jnp.float32, 0.5, 1.5)
    replica_factor = jax.random.uniform(replica_key, (head_groups, 1, 1), jnp.float32, 0.6, 1.4)
    outburst_mask = jax.random.uniform(outburst_key, (head_groups, REPLICA_TOKENS, HEAD_GROUP), jnp.float32) < 3.0 / REPLICA_TOKENS
    outburst_loss = jax.random.uniform(loss_key, (head_groups, REPLICA_TOKENS, HEAD_GROUP), jnp.float32, 0.2, 0.7)
    sampled_values = -per_head_rates[None, None, :] * random_wobble * replica_factor + jnp.where(outburst_mask, jnp.log1p(-outburst_loss), 0.0)
    return sampled_values.reshape(TOKENS, HEAD_GROUP).astype(jnp.float32)


def draw_error_in(key, part):
    key = jax.random.fold_in(key, 11)
    key_noise, key_group, key_sign, key_size, key_rows = jax.random.split(key, 5)
    row_group = jax.random.randint(key_group, (D,), 0, R)
    row_sign = jnp.where(jax.random.bernoulli(key_sign, 0.5, (D,)), 1.0, -1.0).astype(jnp.float32)
    noise = 0.1 * jax.random.truncated_normal(key_noise, -4.0, 4.0, (REPLICAS, D, E), jnp.float32)
    row_size = jnp.exp(jax.random.uniform(key_size, (D,), jnp.float32, math.log(0.3), math.log(3.0)))
    shared_rows = jax.random.truncated_normal(key_rows, -2.5, 2.5, (R, E), jnp.float32)
    common = 0.15 * (row_sign * row_size)[:, None] * jnp.take(shared_rows, row_group, axis=0)
    return (noise + common[None, :, :]).astype(jnp.bfloat16)


def block_levels(own_key, shape, shards, smallest, largest):
    loudness, own = 1.0, jax.random.fold_in(own_key, 6)
    for axis_at, blocks in shards:
        heights = jnp.exp(jax.random.uniform(jax.random.fold_in(own, axis_at), (blocks,), jnp.float32, smallest / len(shards), largest / len(shards)))
        loudness = loudness * jnp.repeat(heights, shape[axis_at] // blocks).reshape([-1 if axis == axis_at else 1 for axis in range(len(shape))])
    return loudness


def normal_values(stream_key, extent, width, reach, shards=(), dtype=jnp.bfloat16):
    array = jax.random.normal(stream_key, extent, jnp.float32) * width
    if len(shards) > 0:
        array = block_levels(stream_key, extent, shards, -0.22, 0.18) * array
    return jnp.clip(array, min=-reach, max=reach).astype(dtype)


def setup_inputs(seed: int = 0) -> dict:
    streams_of = jax.random.split(jax.random.key(seed), 10)
    return {
        "layer_in": normal_values(streams_of[0], (TOKENS, D), 1.0, 6.0, ((0, 128),)),
        "ssm_in": normal_values(streams_of[1], (TOKENS, E), 1.0, 6.0, ((0, 128), (1, 2))),
        "b_in": normal_values(streams_of[2], (TOKENS, NSTATE), 0.25, 1.5, ((0, 128),)),
        "c_in": normal_values(streams_of[3], (TOKENS, NSTATE), 0.25, 1.5, ((0, 128),)),
        "log_decay": draw_log_decay(jax.random.fold_in(streams_of[9], 71), 0),
        "skip_gain": jnp.clip(0.5 + 1.0 * jax.random.uniform(streams_of[5], (HEAD_GROUP,), jnp.float32) ** block_levels(streams_of[5], (HEAD_GROUP,), ((0, 2),), -0.2, 0.2), 0.5, 1.5),
        "grad_out": normal_values(streams_of[6], (TOKENS, E), 1.0, 6.0, ((0, 128), (1, 2))),
        "q_seed": jax.random.randint(streams_of[7], (1,), 0, 46337).astype(jnp.int32),
        "error_in": draw_error_in(jax.random.fold_in(streams_of[9], 71), 0),
    }


def start_factor(q_seed, rank_count, column_count, offset):
    rank_idx = lax.broadcasted_iota(jnp.int32, (rank_count, column_count), 0)
    column_idx = lax.broadcasted_iota(jnp.int32, (rank_count, column_count), 1) + offset
    section_one = (rank_idx * 7919 + column_idx * 104 + q_seed[0]) % 46337
    section_two = section_one * section_one % 46337
    section_three = (section_two * 211 + column_idx * 13 + rank_idx) % 46337
    section_four = section_three * section_three % 46337
    return section_four.astype(jnp.float32) * (2.0 / 46337.0) - 1.0

def scan_forward(inputs, log_decay, b_state, c_state, skip_gain, span_len):
    length_all, head_count, head_width = inputs.shape
    span_count = length_all // span_len
    blocked = inputs.reshape(span_count, span_len, head_count, head_width)
    decays = log_decay.reshape(span_count, span_len, head_count)
    b_blocks = b_state.reshape(span_count, span_len, -1)
    c_blocks = c_state.reshape(span_count, span_len, -1)
    cumulative = jnp.cumsum(decays, axis=1)
    causal = (lax.broadcasted_iota(jnp.int32, (span_len, span_len), 0) >= lax.broadcasted_iota(jnp.int32, (span_len, span_len), 1))[None, :, :, None]
    gaps_log = cumulative[:, :, None, :] - cumulative[:, None, :, :]
    within = jnp.where(causal, jnp.exp(jnp.where(causal, gaps_log, 0.0)), 0.0)
    scores = jnp.einsum('ctn,csn->cts', c_blocks, b_blocks, precision=lax.Precision.HIGHEST)
    inside = jnp.einsum('cts,ctsh,cshp->cthp', scores, within, blocked, precision=lax.Precision.HIGHEST)
    remain = jnp.exp(cumulative[:, -1:, :] - cumulative)
    states = jnp.einsum('csh,cshp,csn->chpn', remain, blocked, b_blocks, precision=lax.Precision.HIGHEST)
    passing = jnp.exp(cumulative[:, -1, :])

    def advance(running, step_in):
        state_new, factor = step_in
        return (running * factor[:, None, None] + state_new, running)
    initial = jnp.zeros(states.shape[1:], jnp.float32)
    _, entering = lax.scan(advance, initial, (states, passing))
    carried = jnp.einsum('cth,ctn,chpn->cthp', jnp.exp(cumulative), c_blocks, entering, precision=lax.Precision.HIGHEST)
    result = inside + carried + skip_gain[None, None, :, None] * blocked
    return result.reshape(length_all, head_count * head_width)

def reference(layer_in, ssm_in, b_in, c_in, log_decay, skip_gain, grad_out, q_seed, error_in):
    columns = E // N_TENSOR
    start = start_factor(q_seed, R, E, 0)

    def replica(step_in):
        rows_in, signal_in, b_rows, c_rows, decay_rows, cotangent, error_rows = step_in

        def forward(signal, b_state, c_state):
            return scan_forward(signal, decay_rows, b_state, c_state, skip_gain, SPAN)
        _, pullback = jax.vjp(forward, signal_in.astype(jnp.float32).reshape(REPLICA_TOKENS, HEAD_GROUP, HEADDIM), b_rows.astype(jnp.float32), c_rows.astype(jnp.float32))
        grad_signal, grad_b, grad_c = pullback(cotangent.astype(jnp.float32))
        rounded = grad_signal.reshape(REPLICA_TOKENS, E).astype(jnp.bfloat16)
        whole = jnp.dot(rows_in.T.astype(jnp.float32), rounded.astype(jnp.float32), preferred_element_type=jnp.float32) / REPLICA_TOKENS
        whole = whole + error_rows.astype(jnp.float32)
        return (whole, jnp.concatenate([grad_b, grad_c], axis=1))
    wholes, grads = lax.map(replica, (layer_in.reshape(N_DP, REPLICA_TOKENS, D), ssm_in.reshape(N_DP, REPLICA_TOKENS, E), b_in.reshape(N_DP, REPLICA_TOKENS, NSTATE), c_in.reshape(N_DP, REPLICA_TOKENS, NSTATE), log_decay.reshape(N_DP, REPLICA_TOKENS, HEAD_GROUP), grad_out.reshape(N_DP, REPLICA_TOKENS, E), error_in))
    split_parts = wholes.reshape(N_DP, D, N_TENSOR, columns)
    starts = start.reshape(R, N_TENSOR, columns)
    psum = jnp.einsum('rke,wdke->krd', starts, split_parts, precision=lax.Precision.HIGHEST)
    gram = jnp.einsum('krd,ksd->krs', psum, psum, precision=lax.Precision.HIGHEST)
    lower = jnp.linalg.cholesky(gram)
    basis = jax.vmap(lambda factor, target: jax.scipy.linalg.solve_triangular(factor, target, lower=True))(lower, psum)
    qsum = jnp.einsum('krd,wdke->rke', basis, split_parts, precision=lax.Precision.HIGHEST)
    correction = jnp.einsum('krd,rke->dke', basis, qsum, precision=lax.Precision.HIGHEST) / N_DP
    error_out = (split_parts - correction[None]).reshape(N_DP, D, E).astype(jnp.bfloat16)
    return (grads.reshape(TOKENS, 2 * NSTATE), basis.reshape(RANKS, D), qsum.reshape(R, E), error_out)
```

```python
import jax
import jax.numpy as jnp
from jax import lax
from jax.experimental import pallas as pl
from jax.experimental.pallas import tpu as pltpu
from jax.sharding import PartitionSpec as P

R = 32
TOK = 768
D = 1280
COLS = 1280
HEADS = 20
N = 128
BLK = 128
NB = TOK // BLK
PAIRS = HEADS // 2
NX, NY, NZ = 4, 4, 8
PR, PC = 8, 384
WIDE = NY * PC
ROWS = 256
F32 = jnp.float32
BF16 = jnp.bfloat16
MESH = pl.DeviceIdType.MESH
VMEM = pltpu.VMEM

NN = (((1,), (0,)), ((), ()))
NT = (((1,), (1,)), ((), ()))
TN = (((0,), (0,)), ((), ()))


def mm(a, b, dims=NN):
    return lax.dot_general(a, b, dims, preferred_element_type=F32)


def split2(v):
    hi = v.astype(BF16)
    lo = (v - hi.astype(F32)).astype(BF16)
    return hi, lo


def split3(v):
    hi = v.astype(BF16)
    rest = v - hi.astype(F32)
    mid = rest.astype(BF16)
    lo = (rest - mid.astype(F32)).astype(BF16)
    return hi, mid, lo


def iota(shape, dim):
    return lax.broadcasted_iota(jnp.int32, shape, dim)


def scan_kernel(
    x_ref, dy_ref, b_ref, c_ref, ld_ref, gain_ref,
    gx_ref, gbc_ref,
    ldp, cum, cum_t, gainp, gain_row, remain, xs, dys, entering, grad_state, passing,
):
    ldp[...] = jnp.zeros((TOK, 128), F32)
    ldp[:, 0:HEADS] = ld_ref[...]
    gainp[...] = jnp.zeros((8, 128), F32)
    gainp[0:1, 0:HEADS] = gain_ref[...]
    expand = (iota((128, COLS), 0) == iota((128, COLS), 1) // 64).astype(BF16)
    expand2 = jnp.concatenate([expand, expand], axis=0)
    gain_hi, gain_mid, gain_lo = split3(gainp[...])
    gain_row[...] = mm(gain_hi, expand) + mm(gain_mid, expand) + mm(gain_lo, expand)
    lower = (iota((BLK, BLK), 0) >= iota((BLK, BLK), 1)).astype(BF16)
    lower3 = jnp.concatenate([lower, lower, lower], axis=1)

    state = jnp.zeros((N, COLS), F32)
    for c in range(NB):
        rows = pl.ds(c * BLK, BLK)
        parts = jnp.concatenate(split3(ldp[rows, :]), axis=0)
        total = mm(lower3, parts)
        cum[rows, :] = total
        cum_t[rows, :] = total.T
        factors = jnp.concatenate([jnp.exp(total), jnp.exp(total[BLK - 1 : BLK, :] - total)], axis=0)
        factors2 = jnp.concatenate(split2(factors), axis=1)
        wide = mm(factors2, expand2)
        grow, left = wide[:BLK], wide[BLK:]
        remain[rows, :] = left
        passing[8 * c : 8 * c + 8, :] = grow[BLK - 8 : BLK]
        x_scaled = (x_ref[rows, :].astype(F32) * left).astype(BF16)
        dy_scaled, dy_rest = split2(dy_ref[rows, :].astype(F32) * grow)
        xs[rows, :] = x_scaled
        dys[rows, :] = dy_scaled
        entering[rows, :] = state.astype(BF16)
        if c < NB - 1:
            state = state * grow[BLK - 1 : BLK] + mm(b_ref[rows, :], x_scaled, TN)
        if c > 0:
            c_blk = c_ref[rows, :]
            grad_state[rows, :] = mm(
                jnp.concatenate([c_blk, c_blk], axis=0), jnp.concatenate([dy_scaled, dy_rest], axis=0), TN
            )

    causal = iota((BLK, BLK), 0) <= iota((BLK, BLK), 1)
    causal2 = jnp.concatenate([causal, causal], axis=1)
    low_half = iota((BLK, 128), 1) < 64
    after = jnp.zeros((N, COLS), F32)
    for c in range(NB - 1, -1, -1):
        rows = pl.ds(c * BLK, BLK)
        b_blk, c_blk = b_ref[rows, :], c_ref[rows, :]
        if c < NB - 1:
            after16, after_rest = split2(after)
            carried = mm(jnp.concatenate([b_blk, b_blk], axis=1), jnp.concatenate([after16, after_rest], axis=0))
            carried = carried * remain[rows, :]
            grad_b = mm(xs[rows, :], after16, NT)
        scores = mm(b_blk, c_blk, NT)
        scores2 = jnp.concatenate([scores, scores], axis=1)
        gaps = jnp.zeros((BLK, BLK), F32)
        for j in range(PAIRS):
            lanes = slice(128 * j, 128 * j + 128)
            dy_pair = dy_ref[rows, lanes]
            zero = jnp.zeros_like(dy_pair)
            both = jnp.concatenate(
                [jnp.where(low_half, dy_pair, zero), jnp.where(low_half, zero, dy_pair)], axis=0
            )
            h = 2 * j
            to_row = jnp.concatenate(
                [cum_t[c * BLK + h : c * BLK + h + 1, :], cum_t[c * BLK + h + 1 : c * BLK + h + 2, :]],
                axis=1,
            )
            from_col = jnp.concatenate(
                [
                    jnp.broadcast_to(cum[rows, h : h + 1], (BLK, BLK)),
                    jnp.broadcast_to(cum[rows, h + 1 : h + 2], (BLK, BLK)),
                ],
                axis=1,
            )
            decay = jnp.exp(jnp.where(causal2, to_row - from_col, -1e30))
            weights, weights_rest = split2(decay * scores2)
            grad_x = mm(weights, both) + mm(weights_rest, both) + gain_row[0:1, lanes] * dy_pair.astype(F32)
            if c < NB - 1:
                grad_x = grad_x + carried[:, lanes]
            gx_ref[rows, lanes] = grad_x.astype(BF16)
            products = mm(x_ref[rows, lanes], both, NT) * decay
            gaps = gaps + products[:, :BLK] + products[:, BLK:]
        gap_hi, gap_lo = split2(gaps)
        grad_b_in = mm(gap_hi, c_blk) + mm(gap_lo, c_blk)
        grad_c = mm(gap_hi, b_blk, TN) + mm(gap_lo, b_blk, TN)
        if c < NB - 1:
            grad_b_in = grad_b_in + grad_b
        if c > 0:
            grad_c = grad_c + mm(dys[rows, :], entering[rows, :], NT)
        gbc_ref[rows, 0:N] = grad_b_in
        gbc_ref[rows, N : 2 * N] = grad_c
        if c > 0:
            after = after * passing[8 * c + 7 : 8 * c + 8, :] + grad_state[rows, :]


def scan_backward(x, dy, b, c, ld, gain):
    vm = pl.BlockSpec(memory_space=VMEM)
    return pl.pallas_call(
        scan_kernel,
        out_shape=(
            jax.ShapeDtypeStruct((TOK, COLS), BF16),
            jax.ShapeDtypeStruct((TOK, 2 * N), F32),
        ),
        in_specs=[vm] * 6,
        out_specs=[vm] * 2,
        scratch_shapes=[
            VMEM((TOK, 128), F32),
            VMEM((TOK, 128), F32),
            VMEM((TOK, 128), F32),
            VMEM((8, 128), F32),
            VMEM((8, COLS), F32),
            VMEM((TOK, COLS), F32),
            VMEM((TOK, COLS), BF16),
            VMEM((TOK, COLS), BF16),
            VMEM((TOK, COLS), BF16),
            VMEM((TOK, COLS), F32),
            VMEM((8 * NB, COLS), F32),
        ],
        compiler_params=pltpu.CompilerParams(vmem_limit_bytes=48 * 1024 * 1024),
        cost_estimate=pl.CostEstimate(
            flops=2 * TOK * COLS * 1024, bytes_accessed=8_000_000, transcendentals=TOK * BLK * HEADS
        ),
    )(x, dy, b, c, ld, gain)


def mod(a):
    quotient = (a.astype(F32) * (1.0 / 46337.0)).astype(jnp.int32)
    left = a - quotient * 46337
    left = jnp.where(left < 0, left + 46337, left)
    return jnp.where(left >= 46337, left - 46337, left)


def start_factor(seed, offset):
    rank = iota((R, COLS), 0)
    column = iota((R, COLS), 1) + offset
    one = mod(rank * 7919 + column * 104 + seed)
    two = mod(one * one)
    three = mod(two * 211 + column * 13 + rank)
    four = mod(three * three)
    return four.astype(F32) * (2.0 / 46337.0) - 1.0


def fold3(v):
    return v[0:R] + v[R : 2 * R] + v[2 * R : 3 * R]


def stack3(v):
    return jnp.concatenate(split3(v), axis=0)


def inverse_factor(gram):
    work = jnp.concatenate(
        [gram, (iota((R, R), 0) == iota((R, R), 1)).astype(F32), jnp.zeros((R, 128 - 2 * R), F32)], axis=1
    )
    row_at = iota((R, 128), 0)
    diag = jnp.ones((R, 128), F32)
    for k in range(R):
        column = jnp.broadcast_to(work[:, k : k + 1], (R, 128))
        pivot = column[k : k + 1, :]
        diag = jnp.where(row_at == k, pivot, diag)
        scaled = work[k : k + 1, :] / pivot
        work = work - jnp.where(row_at > k, column, 0.0) * scaled
    return (work * lax.rsqrt(diag))[:, R : 2 * R]


class Comm:
    def __init__(self, local, full, slots, line, sems):
        self.local, self.full, self.slots, self.line, self.sems = local, full, slots, line, sems
        at = lax.axis_index("dp")
        self.core = lax.axis_index("tensor")
        self.x = lax.rem(at, NX)
        self.z = lax.rem(at // NX, NZ)
        self.y = at // (NX * NZ)

    def device(self, y, z, x):
        return ((y * NZ + z) * NX + x, self.core)

    def neighbour(self, k):
        return lax.rem(self.y + k // NX, NY), lax.rem(self.x + k % NX, NX)

    def piece(self, ref, y, x):
        return ref.at[pl.ds(pl.multiple_of(x * PR, PR), PR), pl.ds(pl.multiple_of(y * PC, 128), PC)]

    def scatter(self, k):
        y, x = self.neighbour(k)
        return pltpu.make_async_remote_copy(
            src_ref=self.piece(self.local, y, x),
            dst_ref=self.slots.at[k],
            send_sem=self.sems.at[0, k],
            recv_sem=self.sems.at[1, k],
            device_id=self.device(y, self.z, x),
            device_id_type=MESH,
        )

    def along(self, k):
        return pltpu.make_async_remote_copy(
            src_ref=self.line.at[self.z],
            dst_ref=self.line.at[self.z],
            send_sem=self.sems.at[2, k],
            recv_sem=self.sems.at[3, k],
            device_id=self.device(self.y, lax.rem(self.z + k, NZ), self.x),
            device_id_type=MESH,
        )

    def gather(self, k):
        y, x = self.neighbour(k)
        mine = self.piece(self.full, self.y, self.x)
        return pltpu.make_async_remote_copy(
            src_ref=mine,
            dst_ref=mine,
            send_sem=self.sems.at[4, k],
            recv_sem=self.sems.at[5, k],
            device_id=self.device(y, self.z, x),
            device_id_type=MESH,
        )

    def begin(self):
        for k in range(1, NX * NY):
            self.scatter(k).start()

    def middle(self):
        total = self.piece(self.local, self.y, self.x)[...]
        for k in range(1, NX * NY):
            self.scatter(k).wait_recv()
            total = total + self.slots[k]
        self.line[self.z] = total
        for k in range(1, NZ):
            self.along(k).start()

    def last(self):
        for k in range(1, NZ):
            self.along(k).wait_recv()
        total = self.line[0]
        for k in range(1, NZ):
            total = total + self.line[k]
        self.piece(self.full, self.y, self.x)[...] = total
        for k in range(1, NX * NY):
            self.gather(k).start()

    def end(self):
        for k in range(1, NX * NY):
            self.gather(k).wait_recv()

    def settle(self):
        for k in range(1, NX * NY):
            self.scatter(k).wait_send()
            self.gather(k).wait_send()
        for k in range(1, NZ):
            self.along(k).wait_send()


def compress_kernel(
    seed_ref, feat_ref, gx_ref, err_ref, gbc_ref,
    gbc_out, p_out, q_out, err_out,
    whole, done, other, local_p, full_p, slots_p, line_p, local_q, full_q, slots_q, line_q,
    sems_p, sems_q, pair_sems, out_sems,
):
    first = Comm(local_p, full_p, slots_p, line_p, sems_p)
    second = Comm(local_q, full_q, slots_q, line_q, sems_q)
    core = first.core
    at = lax.axis_index("dp")

    barrier = pltpu.get_barrier_semaphore()
    for k in range(1, NX * NY):
        y, x = first.neighbour(k)
        pl.semaphore_signal(barrier, inc=1, device_id=first.device(y, first.z, x), device_id_type=MESH)
    for k in range(1, NZ):
        pl.semaphore_signal(
            barrier, inc=1, device_id=first.device(first.y, lax.rem(first.z + k, NZ), first.x), device_id_type=MESH
        )
    pl.semaphore_signal(barrier, inc=1, device_id=(at, 1 - core), device_id_type=MESH)

    local_p[:, D:] = jnp.zeros((R, WIDE - D), F32)
    local_q[:, D:] = jnp.zeros((R, WIDE - D), F32)
    start = stack3(start_factor(seed_ref[0], core * COLS))
    through = fold3(mm(start, gx_ref[...], NT))
    own = mm(stack3(through), feat_ref[...]) * (1.0 / TOK) + mm(start, err_ref[...], NT)
    local_p[:, :D] = fold3(own)

    pl.semaphore_wait(barrier, NX * NY - 1 + NZ - 1 + 1)
    first.begin()
    swap = pltpu.make_async_remote_copy(
        src_ref=gbc_ref,
        dst_ref=other,
        send_sem=pair_sems.at[0],
        recv_sem=pair_sems.at[1],
        device_id=(at, 1 - core),
        device_id_type=MESH,
    )
    swap.start()

    def whole_rows(i):
        rows = pl.ds(i * ROWS, ROWS)
        part = mm(feat_ref[:, i * ROWS : (i + 1) * ROWS], gx_ref[...], TN)
        whole[rows, :] = part * (1.0 / TOK) + err_ref[rows, :].astype(F32)

    whole_rows(0)
    first.middle()
    whole_rows(1)
    first.last()
    whole_rows(2)
    first.end()

    psum = full_p[:, :D]
    parts = stack3(psum)
    cross = mm(parts, parts, NT)
    gram = jnp.zeros((R, R), F32)
    for a in range(2, -1, -1):
        for b in range(2, -1, -1):
            gram = gram + cross[R * a : R * a + R, R * b : R * b + R]
    inverse = inverse_factor(gram)
    basis = lax.dot_general(inverse, psum, NN, precision=lax.Precision.HIGHEST, preferred_element_type=F32)
    p_out[...] = basis
    basis3 = stack3(basis)
    through = fold3(mm(basis3, feat_ref[...], NT))
    own = mm(stack3(through), gx_ref[...]) * (1.0 / TOK) + mm(basis3, err_ref[...])
    local_q[:, :COLS] = fold3(own)

    second.begin()
    whole_rows(3)
    second.middle()
    whole_rows(4)
    second.last()
    swap.wait()
    gbc_out[...] = gbc_ref[...] + other[...]
    second.end()

    summed = full_q[:, :COLS]
    q_out[...] = summed
    q_hi, q_lo = split2(summed)
    p_hi, p_lo = split2(basis * (1.0 / 128.0))
    left = jnp.concatenate([p_hi, p_hi, p_lo, p_lo], axis=0)
    right = jnp.concatenate([q_hi, q_lo, q_hi, q_lo], axis=0)
    copies = []
    for i in range(D // ROWS):
        rows = pl.ds(i * ROWS, ROWS)
        correction = mm(left[:, i * ROWS : (i + 1) * ROWS], right, TN)
        done[rows, :] = (whole[rows, :] - correction).astype(BF16)
        copy = pltpu.make_async_copy(done.at[rows, :], err_out.at[0, rows, :], out_sems.at[i])
        copy.start()
        copies.append(copy)
    first.settle()
    second.settle()
    for copy in copies:
        copy.wait()


def compress(seed, feat, gx, err, gbc):
    vm = pl.BlockSpec(memory_space=VMEM)
    piece = VMEM((R, WIDE), F32)
    slots = VMEM((NX * NY, PR, PC), F32)
    line = VMEM((NZ, PR, PC), F32)
    return pl.pallas_call(
        compress_kernel,
        out_shape=(
            jax.ShapeDtypeStruct((TOK, 2 * N), F32),
            jax.ShapeDtypeStruct((R, D), F32),
            jax.ShapeDtypeStruct((R, COLS), F32),
            jax.ShapeDtypeStruct((1, D, COLS), BF16),
        ),
        in_specs=[pl.BlockSpec(memory_space=pltpu.SMEM), vm, vm, vm, vm],
        out_specs=[vm, vm, vm, pl.BlockSpec(memory_space=pl.ANY)],
        scratch_shapes=[
            VMEM((D, COLS), F32),
            VMEM((D, COLS), BF16),
            VMEM((TOK, 2 * N), F32),
            piece, piece, slots, line,
            piece, piece, slots, line,
            pltpu.SemaphoreType.DMA((6, NX * NY)),
            pltpu.SemaphoreType.DMA((6, NX * NY)),
            pltpu.SemaphoreType.DMA((2,)),
            pltpu.SemaphoreType.DMA((D // ROWS,)),
        ],
        compiler_params=pltpu.CompilerParams(
            collective_id=0, has_side_effects=True, vmem_limit_bytes=48 * 1024 * 1024
        ),
        cost_estimate=pl.CostEstimate(
            flops=2 * D * COLS * 1100, bytes_accessed=14_000_000, transcendentals=0
        ),
    )(seed, feat, gx, err, gbc)


def body(layer_in, ssm_in, b_in, c_in, log_decay, skip_gain, grad_out, q_seed, error_in):
    gx, gbc = scan_backward(ssm_in, grad_out, b_in, c_in, log_decay, skip_gain.reshape(1, HEADS))
    return compress(q_seed, layer_in, gx, error_in.reshape(D, COLS), gbc)


def solution(mesh):
    in_specs = (
        P("dp", None),
        P("dp", "tensor"),
        P("dp", None),
        P("dp", None),
        P("dp", "tensor"),
        P("tensor"),
        P("dp", "tensor"),
        P(),
        P("dp", None, "tensor"),
    )
    out_specs = (P("dp", None), P("tensor", None), P(None, "tensor"), P("dp", None, "tensor"))
    return jax.shard_map(body, mesh=mesh, in_specs=in_specs, out_specs=out_specs, check_vma=False)
```

```python
import jax
import jax.numpy as jnp
from jax import lax
from jax.experimental import pallas as pl
from jax.experimental.pallas import tpu as pltpu
from jax.sharding import PartitionSpec as P

R = 32
TOK = 768
D = 1280
COLS = 1280
HEADS = 20
N = 128
BLK = 128
NB = TOK // BLK
PAIRS = HEADS // 2
NX, NY, NZ = 4, 4, 8
PLANE = NX * NY
PR, PC = 8, 384
WIDE = NY * PC
ROWS = 256
F32 = jnp.float32
BF16 = jnp.bfloat16
MESH = pl.DeviceIdType.MESH
VMEM = pltpu.VMEM
MIB = 1024 * 1024

NN = (((1,), (0,)), ((), ()))
NT = (((1,), (1,)), ((), ()))
TN = (((0,), (0,)), ((), ()))


def hops(k, size):
    return min(k, size - k)


IN_PLANE = sorted(range(1, PLANE), key=lambda k: -hops(k // NX, NY) - hops(k % NX, NX))
ON_LINE = sorted(range(1, NZ), key=lambda k: -hops(k, NZ))


def mm(a, b, dims=NN):
    return lax.dot_general(a, b, dims, preferred_element_type=F32)


def exact(a, b):
    return lax.dot_general(a, b, NN, precision=lax.Precision.HIGHEST, preferred_element_type=F32)


def split2(v):
    hi = v.astype(BF16)
    lo = (v - hi.astype(F32)).astype(BF16)
    return hi, lo


def split3(v):
    hi = v.astype(BF16)
    rest = v - hi.astype(F32)
    mid = rest.astype(BF16)
    lo = (rest - mid.astype(F32)).astype(BF16)
    return hi, mid, lo


def stack3(v):
    return jnp.concatenate(split3(v), axis=0)


def fold3(v):
    return v[0:R] + v[R : 2 * R] + v[2 * R : 3 * R]


def iota(shape, dim):
    return lax.broadcasted_iota(jnp.int32, shape, dim)


def block(c):
    return pl.ds(pl.multiple_of(c * BLK, BLK), BLK)


def mod(a):
    quotient = (a.astype(F32) * (1.0 / 46337.0)).astype(jnp.int32)
    left = a - quotient * 46337
    left = jnp.where(left < 0, left + 46337, left)
    return jnp.where(left >= 46337, left - 46337, left)


def start_factor(seed, offset):
    rank = iota((R, COLS), 0)
    column = iota((R, COLS), 1) + offset
    one = mod(rank * 7919 + column * 104 + seed)
    two = mod(one * one)
    three = mod(two * 211 + column * 13 + rank)
    four = mod(three * three)
    return four.astype(F32) * (2.0 / 46337.0) - 1.0


def inverse_factor(gram):
    work = jnp.concatenate(
        [gram, (iota((R, R), 0) == iota((R, R), 1)).astype(F32), jnp.zeros((R, 128 - 2 * R), F32)], axis=1
    )
    row_at = iota((R, 128), 0)
    diag = jnp.ones((R, 128), F32)
    for k in range(R):
        column = jnp.broadcast_to(work[:, k : k + 1], (R, 128))
        pivot = column[k : k + 1, :]
        diag = jnp.where(row_at == k, pivot, diag)
        scaled = work[k : k + 1, :] / pivot
        work = work - jnp.where(row_at > k, column, 0.0) * scaled
    return (work * lax.rsqrt(diag))[:, R : 2 * R]


class Comm:
    def __init__(self, local, full, slots, line, sems):
        self.local, self.full, self.slots, self.line, self.sems = local, full, slots, line, sems
        at = lax.axis_index("dp")
        self.core = lax.axis_index("tensor")
        self.x = lax.rem(at, NX)
        self.z = lax.rem(at // NX, NZ)
        self.y = at // (NX * NZ)

    def device(self, y, z, x):
        return ((y * NZ + z) * NX + x, self.core)

    def neighbour(self, k):
        return lax.rem(self.y + k // NX, NY), lax.rem(self.x + k % NX, NX)

    def greet(self, barrier):
        for k in IN_PLANE:
            y, x = self.neighbour(k)
            pl.semaphore_signal(barrier, inc=1, device_id=self.device(y, self.z, x), device_id_type=MESH)
        for k in ON_LINE:
            z = lax.rem(self.z + k, NZ)
            pl.semaphore_signal(barrier, inc=1, device_id=self.device(self.y, z, self.x), device_id_type=MESH)

    def piece(self, ref, y, x):
        return ref.at[pl.ds(pl.multiple_of(x * PR, PR), PR), pl.ds(pl.multiple_of(y * PC, 128), PC)]

    def scatter(self, k):
        y, x = self.neighbour(k)
        return pltpu.make_async_remote_copy(
            src_ref=self.piece(self.local, y, x),
            dst_ref=self.slots.at[k],
            send_sem=self.sems.at[0, k],
            recv_sem=self.sems.at[1, k],
            device_id=self.device(y, self.z, x),
            device_id_type=MESH,
        )

    def along(self, k):
        return pltpu.make_async_remote_copy(
            src_ref=self.line.at[self.z],
            dst_ref=self.line.at[self.z],
            send_sem=self.sems.at[2, k],
            recv_sem=self.sems.at[3, k],
            device_id=self.device(self.y, lax.rem(self.z + k, NZ), self.x),
            device_id_type=MESH,
        )

    def gather(self, k):
        y, x = self.neighbour(k)
        mine = self.piece(self.full, self.y, self.x)
        return pltpu.make_async_remote_copy(
            src_ref=mine,
            dst_ref=mine,
            send_sem=self.sems.at[4, k],
            recv_sem=self.sems.at[5, k],
            device_id=self.device(y, self.z, x),
            device_id_type=MESH,
        )

    def begin(self):
        for k in IN_PLANE:
            self.scatter(k).start()

    def middle(self):
        total = self.piece(self.local, self.y, self.x)[...]
        for k in IN_PLANE[::-1]:
            self.scatter(k).wait_recv()
            total = total + self.slots[k]
        self.line[self.z] = total
        for k in ON_LINE:
            self.along(k).start()

    def last(self):
        for k in ON_LINE[::-1]:
            self.along(k).wait_recv()
        total = self.line[0]
        for k in range(1, NZ):
            total = total + self.line[k]
        self.piece(self.full, self.y, self.x)[...] = total
        for k in IN_PLANE:
            self.gather(k).start()

    def end(self):
        for k in IN_PLANE[::-1]:
            self.gather(k).wait_recv()

    def settle(self):
        for k in IN_PLANE:
            self.scatter(k).wait_send()
            self.gather(k).wait_send()
        for k in ON_LINE:
            self.along(k).wait_send()


def main_kernel(
    seed_ref, feat_hbm, x_hbm, b_hbm, c_hbm, ld_hbm, gain_hbm, dy_hbm, err_hbm,
    whole_hbm, p_out, q_out, gbc_out, left_out, right_out,
    whole, feat, xin, dy, err, b_in, c_in, ld_in, gain_in, gx,
    ldp, gainp, gain_row, remain, decays, dys, after, after16, state, passing,
    start, through, first_part, gbc, other,
    local_p, full_p, slots_p, line_p, local_q, full_q, slots_q, line_q,
    sems_p, sems_q, pair_sems, in_sems, dy_sems, err_sems, whole_sems,
):
    first = Comm(local_p, full_p, slots_p, line_p, sems_p)
    second = Comm(local_q, full_q, slots_q, line_q, sems_q)
    core = first.core
    at = lax.axis_index("dp")

    def dy_copy(c):
        return pltpu.make_async_copy(dy_hbm.at[block(c), :], dy.at[block(c), :], dy_sems.at[c])

    def err_copy(i):
        rows = pl.ds(pl.multiple_of(i * ROWS, ROWS), ROWS)
        return pltpu.make_async_copy(err_hbm.at[rows, :], err.at[rows, :], err_sems.at[i])

    small = [(ld_hbm, ld_in), (b_hbm, b_in), (c_hbm, c_in), (gain_hbm, gain_in)]
    small = [pltpu.make_async_copy(s, d, in_sems.at[i]) for i, (s, d) in enumerate(small)]
    feat_copy = pltpu.make_async_copy(feat_hbm, feat, in_sems.at[4])
    x_copy = pltpu.make_async_copy(x_hbm, xin, in_sems.at[5])
    for copy in small:
        copy.start()
    for c in range(NB - 1, -1, -1):
        dy_copy(c).start()
    for i in range(D // ROWS):
        err_copy(i).start()
    feat_copy.start()
    x_copy.start()

    barrier = pltpu.get_barrier_semaphore()
    first.greet(barrier)
    pl.semaphore_signal(barrier, inc=1, device_id=(at, 1 - core), device_id_type=MESH)

    local_p[:, D:] = jnp.zeros((R, WIDE - D), F32)
    local_q[:, D:] = jnp.zeros((R, WIDE - D), F32)
    ldp[...] = jnp.zeros((128, TOK), F32)
    gainp[...] = jnp.zeros((8, 128), F32)
    after[...] = jnp.zeros((N, COLS), F32)
    state[...] = jnp.zeros((N, COLS), F32)
    start[...] = stack3(start_factor(seed_ref[0], core * COLS))
    expand = (iota((128, COLS), 0) == iota((128, COLS), 1) // 64).astype(BF16)
    expand2 = jnp.concatenate([expand, expand], axis=0)
    lower = (iota((BLK, BLK), 0) >= iota((BLK, BLK), 1)).astype(BF16)
    lower3 = jnp.concatenate([lower, lower, lower], axis=1)
    causal = iota((BLK, BLK), 0) <= iota((BLK, BLK), 1)
    causal2 = jnp.concatenate([causal, causal], axis=1)
    low_half = iota((BLK, 128), 1) < 64

    for copy in small:
        copy.wait()
    ldp[0:HEADS, :] = ld_in[...]
    gainp[0:1, 0:HEADS] = gain_in[...]
    gain_hi, gain_mid, gain_lo = split3(gainp[...])
    gain_row[...] = mm(gain_hi, expand) + mm(gain_mid, expand) + mm(gain_lo, expand)

    def masked(dy_pair):
        zero = jnp.zeros_like(dy_pair)
        return jnp.concatenate([jnp.where(low_half, dy_pair, zero), jnp.where(low_half, zero, dy_pair)], axis=0)

    def token_block(c, more):
        rows = block(c)
        dy_copy(c).wait()
        turned = mm(jnp.concatenate(split3(ldp[:, rows]), axis=1), lower3, NT)
        total = turned.T
        factors = jnp.concatenate([jnp.exp(total), jnp.exp(total[BLK - 1 : BLK, :] - total)], axis=0)
        wide = mm(jnp.concatenate(split2(factors), axis=1), expand2)
        grow, left = wide[:BLK], wide[BLK:]
        remain[rows, :] = left
        passing[pl.ds(pl.multiple_of(8 * c, 8), 8), :] = grow[BLK - 8 : BLK]
        dy_scaled, dy_rest = split2(dy[rows, :].astype(F32) * grow)
        dys[rows, :] = dy_scaled
        b_blk, c_blk = b_in[rows, :], c_in[rows, :]
        now = after[...]
        now16, now_rest = split2(now)
        after16[rows, :] = now16
        carried = mm(jnp.concatenate([b_blk, b_blk], axis=1), jnp.concatenate([now16, now_rest], axis=0)) * left
        scores = mm(b_blk, c_blk, NT)
        scores2 = jnp.concatenate([scores, scores], axis=1)
        for j in range(PAIRS):
            lanes = slice(128 * j, 128 * j + 128)
            dy_pair = dy[rows, lanes]
            both = masked(dy_pair)
            h = 2 * j
            to_row = jnp.concatenate([turned[h : h + 1, :], turned[h + 1 : h + 2, :]], axis=1)
            from_col = jnp.concatenate(
                [
                    jnp.broadcast_to(total[:, h : h + 1], (BLK, BLK)),
                    jnp.broadcast_to(total[:, h + 1 : h + 2], (BLK, BLK)),
                ],
                axis=1,
            )
            decay = jnp.exp(jnp.where(causal2, to_row - from_col, -1e30))
            decays[rows, 256 * j : 256 * j + 256] = decay
            weights, weights_rest = split2(decay * scores2)
            grad_x = mm(weights, both) + mm(weights_rest, both)
            grad_x = grad_x + gain_row[0:1, lanes] * dy_pair.astype(F32) + carried[:, lanes]
            gx[rows, lanes] = grad_x.astype(BF16)
        through[:, rows] = fold3(mm(start[...], gx[rows, :], NT))
        if more:
            after[...] = now * grow[BLK - 1 : BLK] + mm(
                jnp.concatenate([c_blk, c_blk], axis=0), jnp.concatenate([dy_scaled, dy_rest], axis=0), TN
            )
            i = NB - 1 - c
            rows = pl.ds(pl.multiple_of(i * ROWS, ROWS), ROWS)
            err_copy(i).wait()
            first_part[:, rows] = fold3(mm(start[...], err[rows, :], NT))

    def step(i, carry):
        token_block(NB - 1 - i, True)
        return carry

    lax.fori_loop(0, NB - 1, step, 0)
    token_block(0, False)
    feat_copy.wait()
    local_p[:, :D] = first_part[...] + fold3(mm(stack3(through[...]), feat[...])) * (1.0 / TOK)

    pl.semaphore_wait(barrier, PLANE - 1 + NZ - 1 + 1)
    first.begin()

    def whole_rows(i):
        rows = pl.ds(i * ROWS, ROWS)
        part = mm(feat[:, i * ROWS : (i + 1) * ROWS], gx[...], TN)
        whole[rows, :] = part * (1.0 / TOK) + err[rows, :].astype(F32)
        copy = pltpu.make_async_copy(whole.at[rows, :], whole_hbm.at[rows, :], whole_sems.at[i])
        copy.start()
        return copy

    def bc_block(c, carry):
        rows = block(c)
        b_blk, c_blk = b_in[rows, :], c_in[rows, :]
        x_scaled = (xin[rows, :].astype(F32) * remain[rows, :]).astype(BF16)
        before = state[...]
        grad_b = mm(x_scaled, after16[rows, :], NT)
        grad_c = mm(dys[rows, :], before.astype(BF16), NT)
        factor = passing[pl.ds(pl.multiple_of(8 * c, 8), 8), :][7:8, :]
        state[...] = before * factor + mm(b_blk, x_scaled, TN)
        gaps = jnp.zeros((BLK, BLK), F32)
        for j in range(PAIRS):
            lanes = slice(128 * j, 128 * j + 128)
            products = mm(xin[rows, lanes], masked(dy[rows, lanes]), NT) * decays[rows, 256 * j : 256 * j + 256]
            gaps = gaps + products[:, :BLK] + products[:, BLK:]
        gap_hi, gap_lo = split2(gaps)
        gbc[rows, 0:N] = grad_b + mm(gap_hi, c_blk) + mm(gap_lo, c_blk)
        gbc[rows, N : 2 * N] = grad_c + mm(gap_hi, b_blk, TN) + mm(gap_lo, b_blk, TN)
        return carry

    whole_copies = [whole_rows(i) for i in range(D // ROWS)]
    first.middle()
    x_copy.wait()
    lax.fori_loop(0, NB // 2, bc_block, 0)
    first.last()
    lax.fori_loop(NB // 2, NB, bc_block, 0)
    swap = pltpu.make_async_remote_copy(
        src_ref=gbc,
        dst_ref=other,
        send_sem=pair_sems.at[0],
        recv_sem=pair_sems.at[1],
        device_id=(at, 1 - core),
        device_id_type=MESH,
    )
    swap.start()
    first.end()

    psum = full_p[:, :D]
    parts = stack3(psum)
    inner = fold3(mm(parts, feat[...], NT))
    local_q[:, :COLS] = fold3(mm(parts, err[...]) + mm(stack3(inner), gx[...]) * (1.0 / TOK))
    second.begin()

    cross = mm(parts, parts, NT)
    gram = jnp.zeros((R, R), F32)
    for a in range(2, -1, -1):
        for b in range(2, -1, -1):
            gram = gram + cross[R * a : R * a + R, R * b : R * b + R]
    inverse = inverse_factor(gram)
    second.middle()

    basis = exact(inverse, psum)
    p_out[...] = basis
    p_hi, p_lo = split2(basis * (1.0 / 128.0))
    left_out[...] = jnp.concatenate([p_hi, p_hi, p_lo, p_lo], axis=0).T
    second.last()

    swap.wait()
    gbc_out[...] = gbc[...] + other[...]
    first.settle()
    second.end()

    summed = exact(inverse, full_q[:, :COLS])
    q_out[...] = summed
    q_hi, q_lo = split2(summed)
    right_out[...] = jnp.concatenate([q_hi, q_lo, q_hi, q_lo], axis=0)
    second.settle()
    for copy in whole_copies:
        copy.wait()


def last_kernel(
    whole_hbm, p_in, q_in, gbc_in, left_hbm, right_hbm, gbc_out, p_out, q_out, err_out,
    whole, left, right, done, p, q, gbc, sems, in_sems, out_sems,
):
    def part(i):
        return pl.ds(i * ROWS, ROWS)

    factors = [
        pltpu.make_async_copy(left_hbm, left, sems.at[0]),
        pltpu.make_async_copy(right_hbm, right, sems.at[1]),
    ]
    loads = [
        pltpu.make_async_copy(whole_hbm.at[part(i), :], whole.at[part(i), :], in_sems.at[i]) for i in range(D // ROWS)
    ]
    passed = [(p_in, p, p_out), (q_in, q, q_out), (gbc_in, gbc, gbc_out)]
    arriving = [pltpu.make_async_copy(v[0], v[1], sems.at[2 + i]) for i, v in enumerate(passed)]
    copies = [pltpu.make_async_copy(v[1], v[2], sems.at[5 + i]) for i, v in enumerate(passed)]
    for copy in factors + loads + arriving:
        copy.start()
    for copy in factors:
        copy.wait()
    for i in range(D // ROWS):
        change = mm(left[part(i), :], right[...])
        loads[i].wait()
        done[part(i), :] = (whole[part(i), :] - change).astype(BF16)
        copy = pltpu.make_async_copy(done.at[part(i), :], err_out.at[0, part(i), :], out_sems.at[i])
        copy.start()
        copies.append(copy)
        if i == 1:
            for into, out in zip(arriving, copies):
                into.wait()
                out.start()
    for copy in copies:
        copy.wait()


def body(layer_in, ssm_in, b_in, c_in, log_decay, skip_gain, grad_out, q_seed, error_in):
    vm = pl.BlockSpec(memory_space=VMEM)
    hbm = pl.BlockSpec(memory_space=pltpu.HBM)
    piece = VMEM((R, WIDE), F32)
    slots = VMEM((PLANE, PR, PC), F32)
    line = VMEM((NZ, PR, PC), F32)
    tokens16 = VMEM((TOK, COLS), BF16)
    tokens32 = VMEM((TOK, COLS), F32)
    dma = pltpu.SemaphoreType.DMA
    whole, p, q, gbc, left, right = pl.pallas_call(
        main_kernel,
        out_shape=(
            jax.ShapeDtypeStruct((D, COLS), F32),
            jax.ShapeDtypeStruct((R, D), F32),
            jax.ShapeDtypeStruct((R, COLS), F32),
            jax.ShapeDtypeStruct((TOK, 2 * N), F32),
            jax.ShapeDtypeStruct((D, 4 * R), BF16),
            jax.ShapeDtypeStruct((4 * R, COLS), BF16),
        ),
        in_specs=[pl.BlockSpec(memory_space=pltpu.SMEM)] + [hbm] * 8,
        out_specs=[hbm] + [vm] * 5,
        scratch_shapes=[
            VMEM((D, COLS), F32),
            tokens16, tokens16, tokens16,
            VMEM((D, COLS), BF16),
            VMEM((TOK, N), BF16), VMEM((TOK, N), BF16),
            VMEM((HEADS, TOK), F32), VMEM((1, HEADS), F32),
            tokens16,
            VMEM((128, TOK), F32),
            VMEM((8, 128), F32), VMEM((8, COLS), F32),
            tokens32,
            VMEM((TOK, HEADS * BLK), F32),
            tokens16,
            VMEM((N, COLS), F32),
            tokens16,
            VMEM((N, COLS), F32),
            VMEM((8 * NB, COLS), F32),
            VMEM((3 * R, COLS), BF16),
            VMEM((R, TOK), F32),
            VMEM((R, D), F32),
            VMEM((TOK, 2 * N), F32), VMEM((TOK, 2 * N), F32),
            piece, piece, slots, line,
            piece, piece, slots, line,
            dma((6, PLANE)), dma((6, PLANE)), dma((2,)), dma((6,)), dma((NB,)), dma((D // ROWS,)), dma((D // ROWS,)),
        ],
        compiler_params=pltpu.CompilerParams(
            collective_id=0, has_side_effects=True, vmem_limit_bytes=62 * MIB
        ),
        cost_estimate=pl.CostEstimate(
            flops=2 * D * COLS * 2200, bytes_accessed=20_000_000, transcendentals=TOK * BLK * HEADS
        ),
    )(
        q_seed, layer_in, ssm_in, b_in, c_in, log_decay.T, skip_gain.reshape(1, HEADS), grad_out,
        error_in.reshape(D, COLS),
    )
    return pl.pallas_call(
        last_kernel,
        out_shape=(
            jax.ShapeDtypeStruct((TOK, 2 * N), F32),
            jax.ShapeDtypeStruct((R, D), F32),
            jax.ShapeDtypeStruct((R, COLS), F32),
            jax.ShapeDtypeStruct((1, D, COLS), BF16),
        ),
        in_specs=[hbm] * 6,
        out_specs=[hbm] * 4,
        scratch_shapes=[
            VMEM((D, COLS), F32), VMEM((D, 4 * R), BF16), VMEM((4 * R, COLS), BF16), VMEM((D, COLS), BF16),
            VMEM((R, D), F32), VMEM((R, COLS), F32), VMEM((TOK, 2 * N), F32), dma((8,)), dma((D // ROWS,)), dma((D // ROWS,)),
        ],
        compiler_params=pltpu.CompilerParams(vmem_limit_bytes=62 * MIB),
        cost_estimate=pl.CostEstimate(flops=2 * D * COLS * 128, bytes_accessed=11_000_000, transcendentals=0),
    )(whole, p, q, gbc, left, right)


def solution(mesh):
    in_specs = (
        P("dp", None),
        P("dp", "tensor"),
        P("dp", None),
        P("dp", None),
        P("dp", "tensor"),
        P("tensor"),
        P("dp", "tensor"),
        P(),
        P("dp", None, "tensor"),
    )
    out_specs = (P("dp", None), P("tensor", None), P(None, "tensor"), P("dp", None, "tensor"))
    return jax.shard_map(body, mesh=mesh, in_specs=in_specs, out_specs=out_specs, check_vma=False)
```

```python
import jax
import jax.numpy as jnp
from jax import lax
from jax.experimental import pallas as pl
from jax.experimental.pallas import tpu as pltpu
from jax.sharding import PartitionSpec as P

R = 32
TOK = 768
D = 1280
COLS = 1280
HEADS = 20
N = 128
BLK = 128
NB = TOK // BLK
PAIRS = HEADS // 2
NX, NY, NZ = 4, 4, 8
PLANE = NX * NY
PR, PC = 8, 384
WIDE = NY * PC
ROWS = 256
F32 = jnp.float32
BF16 = jnp.bfloat16
MESH = pl.DeviceIdType.MESH
VMEM = pltpu.VMEM
MIB = 1024 * 1024

NN = (((1,), (0,)), ((), ()))
NT = (((1,), (1,)), ((), ()))
TN = (((0,), (0,)), ((), ()))


def hops(k, size):
    return min(k, size - k)


IN_PLANE = sorted(range(1, PLANE), key=lambda k: -hops(k // NX, NY) - hops(k % NX, NX))
ON_LINE = sorted(range(1, NZ), key=lambda k: -hops(k, NZ))


def mm(a, b, dims=NN):
    return lax.dot_general(a, b, dims, preferred_element_type=F32)


def exact(a, b):
    return lax.dot_general(a, b, NN, precision=lax.Precision.HIGHEST, preferred_element_type=F32)


def split2(v):
    hi = v.astype(BF16)
    lo = (v - hi.astype(F32)).astype(BF16)
    return hi, lo


def split3(v):
    hi = v.astype(BF16)
    rest = v - hi.astype(F32)
    mid = rest.astype(BF16)
    lo = (rest - mid.astype(F32)).astype(BF16)
    return hi, mid, lo


def stack3(v):
    return jnp.concatenate(split3(v), axis=0)


def fold3(v):
    return v[0:R] + v[R : 2 * R] + v[2 * R : 3 * R]


def iota(shape, dim):
    return lax.broadcasted_iota(jnp.int32, shape, dim)


def block(c):
    return pl.ds(pl.multiple_of(c * BLK, BLK), BLK)


def mod(a):
    quotient = (a.astype(F32) * (1.0 / 46337.0)).astype(jnp.int32)
    left = a - quotient * 46337
    left = jnp.where(left < 0, left + 46337, left)
    return jnp.where(left >= 46337, left - 46337, left)


def start_factor(seed, offset):
    rank = iota((R, COLS), 0)
    column = iota((R, COLS), 1) + offset
    one = mod(rank * 7919 + column * 104 + seed)
    two = mod(one * one)
    three = mod(two * 211 + column * 13 + rank)
    four = mod(three * three)
    return four.astype(F32) * (2.0 / 46337.0) - 1.0


def inverse_factor(gram):
    work = jnp.concatenate(
        [gram, (iota((R, R), 0) == iota((R, R), 1)).astype(F32), jnp.zeros((R, 128 - 2 * R), F32)], axis=1
    )
    row_at = iota((R, 128), 0)
    diag = jnp.ones((R, 128), F32)
    for k in range(R):
        column = jnp.broadcast_to(work[:, k : k + 1], (R, 128))
        pivot = column[k : k + 1, :]
        diag = jnp.where(row_at == k, pivot, diag)
        scaled = work[k : k + 1, :] / pivot
        work = work - jnp.where(row_at > k, column, 0.0) * scaled
    return (work * lax.rsqrt(diag))[:, R : 2 * R]


class Comm:
    def __init__(self, local, full, slots, line, sems):
        self.local, self.full, self.slots, self.line, self.sems = local, full, slots, line, sems
        at = lax.axis_index("dp")
        self.core = lax.axis_index("tensor")
        self.x = lax.rem(at, NX)
        self.z = lax.rem(at // NX, NZ)
        self.y = at // (NX * NZ)

    def device(self, y, z, x):
        return ((y * NZ + z) * NX + x, self.core)

    def neighbour(self, k):
        return lax.rem(self.y + k // NX, NY), lax.rem(self.x + k % NX, NX)

    def greet(self, barrier):
        for k in IN_PLANE:
            y, x = self.neighbour(k)
            pl.semaphore_signal(barrier, inc=1, device_id=self.device(y, self.z, x), device_id_type=MESH)
        for k in ON_LINE:
            z = lax.rem(self.z + k, NZ)
            pl.semaphore_signal(barrier, inc=1, device_id=self.device(self.y, z, self.x), device_id_type=MESH)

    def piece(self, ref, y, x):
        return ref.at[pl.ds(pl.multiple_of(x * PR, PR), PR), pl.ds(pl.multiple_of(y * PC, 128), PC)]

    def scatter(self, k):
        y, x = self.neighbour(k)
        return pltpu.make_async_remote_copy(
            src_ref=self.piece(self.local, y, x),
            dst_ref=self.slots.at[k],
            send_sem=self.sems.at[0, k],
            recv_sem=self.sems.at[1, k],
            device_id=self.device(y, self.z, x),
            device_id_type=MESH,
        )

    def along(self, k):
        return pltpu.make_async_remote_copy(
            src_ref=self.line.at[self.z],
            dst_ref=self.line.at[self.z],
            send_sem=self.sems.at[2, k],
            recv_sem=self.sems.at[3, k],
            device_id=self.device(self.y, lax.rem(self.z + k, NZ), self.x),
            device_id_type=MESH,
        )

    def gather(self, k):
        y, x = self.neighbour(k)
        mine = self.piece(self.full, self.y, self.x)
        return pltpu.make_async_remote_copy(
            src_ref=mine,
            dst_ref=mine,
            send_sem=self.sems.at[4, k],
            recv_sem=self.sems.at[5, k],
            device_id=self.device(y, self.z, x),
            device_id_type=MESH,
        )

    def begin(self):
        for k in IN_PLANE:
            self.scatter(k).start()

    def middle(self):
        total = self.piece(self.local, self.y, self.x)[...]
        for k in IN_PLANE[::-1]:
            self.scatter(k).wait_recv()
            total = total + self.slots[k]
        self.line[self.z] = total
        for k in ON_LINE:
            self.along(k).start()

    def last(self):
        for k in ON_LINE[::-1]:
            self.along(k).wait_recv()
        total = self.line[0]
        for k in range(1, NZ):
            total = total + self.line[k]
        self.piece(self.full, self.y, self.x)[...] = total
        for k in IN_PLANE:
            self.gather(k).start()

    def end(self):
        for k in IN_PLANE[::-1]:
            self.gather(k).wait_recv()

    def settle(self):
        for k in IN_PLANE:
            self.scatter(k).wait_send()
            self.gather(k).wait_send()
        for k in ON_LINE:
            self.along(k).wait_send()


def main_kernel(
    seed_ref, feat_hbm, x_hbm, b_hbm, c_hbm, ld_hbm, gain_hbm, dy_hbm, err_hbm,
    whole, p_out, q_out, gbc_out, left_out, right_out,
    feat, xin, dy, err, b_in, c_in, ld_in, gain_in, gx,
    ldp, gainp, gain_row, remain, decays, dys, after, after16, state, passing,
    start, first_part, gbc, other,
    local_p, full_p, slots_p, line_p, local_q, full_q, slots_q, line_q,
    sems_p, sems_q, pair_sems, in_sems, dy_sems, err_sems,
):
    first = Comm(local_p, full_p, slots_p, line_p, sems_p)
    second = Comm(local_q, full_q, slots_q, line_q, sems_q)
    core = first.core
    at = lax.axis_index("dp")

    def dy_copy(c):
        return pltpu.make_async_copy(dy_hbm.at[block(c), :], dy.at[block(c), :], dy_sems.at[c])

    def err_copy(i):
        rows = pl.ds(pl.multiple_of(i * ROWS, ROWS), ROWS)
        return pltpu.make_async_copy(err_hbm.at[rows, :], err.at[rows, :], err_sems.at[i])

    small = [(ld_hbm, ld_in), (b_hbm, b_in), (c_hbm, c_in), (gain_hbm, gain_in)]
    small = [pltpu.make_async_copy(s, d, in_sems.at[i]) for i, (s, d) in enumerate(small)]
    feat_copy = pltpu.make_async_copy(feat_hbm, feat, in_sems.at[4])
    x_copy = pltpu.make_async_copy(x_hbm, xin, in_sems.at[5])
    for copy in small:
        copy.start()
    dy_copy(NB - 1).start()

    barrier = pltpu.get_barrier_semaphore()
    first.greet(barrier)
    pl.semaphore_signal(barrier, inc=1, device_id=(at, 1 - core), device_id_type=MESH)

    local_p[:, D:] = jnp.zeros((R, WIDE - D), F32)
    local_q[:, D:] = jnp.zeros((R, WIDE - D), F32)
    ldp[...] = jnp.zeros((128, TOK), F32)
    gainp[...] = jnp.zeros((8, 128), F32)
    after[...] = jnp.zeros((N, COLS), F32)
    state[...] = jnp.zeros((N, COLS), F32)
    factor3 = stack3(start_factor(seed_ref[0], core * COLS))
    start[...] = jnp.concatenate([factor3, jnp.zeros((R, COLS), BF16)], axis=0).T
    expand = (iota((128, COLS), 0) == iota((128, COLS), 1) // 64).astype(BF16)
    expand2 = jnp.concatenate([expand, expand], axis=0)
    lower = (iota((BLK, BLK), 0) >= iota((BLK, BLK), 1)).astype(BF16)
    lower3 = jnp.concatenate([lower, lower, lower], axis=1)
    causal = iota((BLK, BLK), 0) <= iota((BLK, BLK), 1)
    causal2 = jnp.concatenate([causal, causal], axis=1)
    low_half = iota((BLK, 128), 1) < 64

    for copy in small:
        copy.wait()
    for c in range(NB - 2, -1, -1):
        dy_copy(c).start()
    for i in range(D // ROWS):
        err_copy(i).start()
    feat_copy.start()
    x_copy.start()
    ldp[0:HEADS, :] = ld_in[...]
    gainp[0:1, 0:HEADS] = gain_in[...]
    gain_hi, gain_mid, gain_lo = split3(gainp[...])
    gain_row[...] = mm(gain_hi, expand) + mm(gain_mid, expand) + mm(gain_lo, expand)

    def masked(dy_pair):
        zero = jnp.zeros_like(dy_pair)
        return jnp.concatenate([jnp.where(low_half, dy_pair, zero), jnp.where(low_half, zero, dy_pair)], axis=0)

    def token_block(c, more):
        rows = block(c)
        turned = mm(jnp.concatenate(split3(ldp[:, rows]), axis=1), lower3, NT)
        total = turned.T
        factors = jnp.concatenate([jnp.exp(total), jnp.exp(total[BLK - 1 : BLK, :] - total)], axis=0)
        wide = mm(jnp.concatenate(split2(factors), axis=1), expand2)
        grow, left = wide[:BLK], wide[BLK:]
        remain[rows, :] = left
        passing[pl.ds(pl.multiple_of(8 * c, 8), 8), :] = grow[BLK - 8 : BLK]
        dy_scaled, dy_rest = split2(dy[rows, :].astype(F32) * grow)
        dys[rows, :] = dy_scaled
        b_blk, c_blk = b_in[rows, :], c_in[rows, :]
        now = after[...]
        now16, now_rest = split2(now)
        after16[rows, :] = now16
        carried = mm(jnp.concatenate([b_blk, b_blk], axis=1), jnp.concatenate([now16, now_rest], axis=0)) * left
        scores = mm(b_blk, c_blk, NT)
        scores2 = jnp.concatenate([scores, scores], axis=1)
        for j in range(PAIRS):
            lanes = slice(128 * j, 128 * j + 128)
            dy_pair = dy[rows, lanes]
            both = masked(dy_pair)
            h = 2 * j
            to_row = jnp.concatenate([turned[h : h + 1, :], turned[h + 1 : h + 2, :]], axis=1)
            from_col = jnp.concatenate(
                [
                    jnp.broadcast_to(total[:, h : h + 1], (BLK, BLK)),
                    jnp.broadcast_to(total[:, h + 1 : h + 2], (BLK, BLK)),
                ],
                axis=1,
            )
            decay = jnp.exp(jnp.where(causal2, to_row - from_col, -1e30))
            decays[rows, 256 * j : 256 * j + 256] = decay
            weights, weights_rest = split2(decay * scores2)
            grad_x = mm(weights, both) + mm(weights_rest, both)
            grad_x = grad_x + gain_row[0:1, lanes] * dy_pair.astype(F32) + carried[:, lanes]
            gx[rows, lanes] = grad_x.astype(BF16)
        if more:
            after[...] = now * grow[BLK - 1 : BLK] + mm(
                jnp.concatenate([c_blk, c_blk], axis=0), jnp.concatenate([dy_scaled, dy_rest], axis=0), TN
            )

    def project(low, high):
        rows = slice(low * BLK, high * BLK)
        return fold3(mm(stack3(fold3(mm(gx[rows, :], start[...]).T)), feat[rows, :]))

    for c in range(NB - 1, -1, -1):
        if c >= NB - 2:
            dy_copy(c).wait()
        elif c == NB - 3:
            for k in range(NB - 3, -1, -1):
                dy_copy(k).wait()
            for i in range(D // ROWS):
                err_copy(i).wait()
        elif c == 0:
            feat_copy.wait()
            early = project(1, NB)
        token_block(c, c > 0)
        if NB - 3 >= c > 0:
            for i in range(2 * (NB - 3 - c), min(2 * (NB - 3 - c) + 2, D // ROWS)):
                rows = pl.ds(i * ROWS, ROWS)
                first_part[:, rows] = fold3(mm(err[rows, :], start[...]).T)
    local_p[:, :D] = first_part[...] + (early + project(0, 1)) * (1.0 / TOK)

    pl.semaphore_wait(barrier, PLANE - 1 + NZ - 1 + 1)
    first.begin()

    def whole_rows(i):
        rows = pl.ds(i * ROWS, ROWS)
        part = mm(feat[:, i * ROWS : (i + 1) * ROWS], gx[...], TN)
        whole[rows, :] = part * (1.0 / TOK) + err[rows, :].astype(F32)

    def bc_block(c, carry):
        rows = block(c)
        b_blk, c_blk = b_in[rows, :], c_in[rows, :]
        x_scaled = (xin[rows, :].astype(F32) * remain[rows, :]).astype(BF16)
        before = state[...]
        grad_b = mm(x_scaled, after16[rows, :], NT)
        grad_c = mm(dys[rows, :], before.astype(BF16), NT)
        factor = passing[pl.ds(pl.multiple_of(8 * c, 8), 8), :][7:8, :]
        state[...] = before * factor + mm(b_blk, x_scaled, TN)
        gaps = jnp.zeros((BLK, BLK), F32)
        for j in range(PAIRS):
            lanes = slice(128 * j, 128 * j + 128)
            products = mm(xin[rows, lanes], masked(dy[rows, lanes]), NT) * decays[rows, 256 * j : 256 * j + 256]
            gaps = gaps + products[:, :BLK] + products[:, BLK:]
        gap_hi, gap_lo = split2(gaps)
        gbc[rows, 0:N] = grad_b + mm(gap_hi, c_blk) + mm(gap_lo, c_blk)
        gbc[rows, N : 2 * N] = grad_c + mm(gap_hi, b_blk, TN) + mm(gap_lo, b_blk, TN)
        return carry

    for i in range(D // ROWS):
        whole_rows(i)
    first.middle()
    x_copy.wait()
    lax.fori_loop(0, NB // 2, bc_block, 0)
    first.last()
    lax.fori_loop(NB // 2, NB, bc_block, 0)
    swap = pltpu.make_async_remote_copy(
        src_ref=gbc,
        dst_ref=other,
        send_sem=pair_sems.at[0],
        recv_sem=pair_sems.at[1],
        device_id=(at, 1 - core),
        device_id_type=MESH,
    )
    swap.start()
    first.end()

    psum = full_p[:, :D]
    parts = stack3(psum)
    inner = fold3(mm(parts, feat[...], NT))
    local_q[:, :COLS] = fold3(mm(parts, err[...]) + mm(stack3(inner), gx[...]) * (1.0 / TOK))
    second.begin()

    cross = mm(parts, parts, NT)
    gram = jnp.zeros((R, R), F32)
    for a in range(2, -1, -1):
        for b in range(2, -1, -1):
            gram = gram + cross[R * a : R * a + R, R * b : R * b + R]
    inverse = inverse_factor(gram)
    second.middle()

    basis = exact(inverse, psum)
    p_out[...] = basis
    p_hi, p_lo = split2(basis * (1.0 / 128.0))
    left_out[...] = jnp.concatenate([p_hi, p_hi, p_lo, p_lo], axis=0).T
    second.last()

    swap.wait()
    gbc_out[...] = gbc[...] + other[...]
    first.settle()
    second.end()

    summed = exact(inverse, full_q[:, :COLS])
    q_out[...] = summed
    q_hi, q_lo = split2(summed)
    right_out[...] = jnp.concatenate([q_hi, q_lo, q_hi, q_lo], axis=0)
    second.settle()


def last_kernel(whole, p_in, q_in, gbc_in, left, right, gbc_out, p_out, q_out, err_out, done, sems, out_sems):
    copies = [
        pltpu.make_async_copy(gbc_in, gbc_out, sems.at[0]),
        pltpu.make_async_copy(p_in, p_out, sems.at[1]),
        pltpu.make_async_copy(q_in, q_out, sems.at[2]),
    ]
    for copy in copies:
        copy.start()
    for i in range(D // ROWS):
        rows = pl.ds(i * ROWS, ROWS)
        done[rows, :] = (whole[rows, :] - mm(left[rows, :], right[...])).astype(BF16)
        copy = pltpu.make_async_copy(done.at[rows, :], err_out.at[0, rows, :], out_sems.at[i])
        copy.start()
        copies.append(copy)
    for copy in copies:
        copy.wait()


def body(layer_in, ssm_in, b_in, c_in, log_decay, skip_gain, grad_out, q_seed, error_in):
    vm = pl.BlockSpec(memory_space=VMEM)
    hbm = pl.BlockSpec(memory_space=pltpu.HBM)
    piece = VMEM((R, WIDE), F32)
    slots = VMEM((PLANE, PR, PC), F32)
    line = VMEM((NZ, PR, PC), F32)
    tokens16 = VMEM((TOK, COLS), BF16)
    tokens32 = VMEM((TOK, COLS), F32)
    dma = pltpu.SemaphoreType.DMA
    held = pl.pallas_call(
        main_kernel,
        out_shape=(
            VMEM((D, COLS), F32),
            VMEM((R, D), F32),
            VMEM((R, COLS), F32),
            VMEM((TOK, 2 * N), F32),
            VMEM((D, 4 * R), BF16),
            VMEM((4 * R, COLS), BF16),
        ),
        in_specs=[pl.BlockSpec(memory_space=pltpu.SMEM)] + [hbm] * 8,
        out_specs=[vm] * 6,
        scratch_shapes=[
            tokens16, tokens16, tokens16,
            VMEM((D, COLS), BF16),
            VMEM((TOK, N), BF16), VMEM((TOK, N), BF16),
            VMEM((HEADS, TOK), F32), VMEM((1, HEADS), F32),
            tokens16,
            VMEM((128, TOK), F32),
            VMEM((8, 128), F32), VMEM((8, COLS), F32),
            tokens32,
            VMEM((TOK, HEADS * BLK), F32),
            tokens16,
            VMEM((N, COLS), F32),
            tokens16,
            VMEM((N, COLS), F32),
            VMEM((8 * NB, COLS), F32),
            VMEM((COLS, 4 * R), BF16),
            VMEM((R, D), F32),
            VMEM((TOK, 2 * N), F32), VMEM((TOK, 2 * N), F32),
            piece, piece, slots, line,
            piece, piece, slots, line,
            dma((6, PLANE)), dma((6, PLANE)), dma((2,)), dma((6,)), dma((NB,)), dma((D // ROWS,)),
        ],
        compiler_params=pltpu.CompilerParams(
            collective_id=0, has_side_effects=True, vmem_limit_bytes=44 * MIB
        ),
        cost_estimate=pl.CostEstimate(
            flops=2 * D * COLS * 2200, bytes_accessed=20_000_000, transcendentals=TOK * BLK * HEADS
        ),
    )(
        q_seed,
        *(
            pltpu.with_memory_space_constraint(v, pltpu.HBM)
            for v in (
                layer_in, ssm_in, b_in, c_in, log_decay.T, skip_gain.reshape(1, HEADS), grad_out,
                error_in.reshape(D, COLS),
            )
        ),
    )
    return pl.pallas_call(
        last_kernel,
        out_shape=(
            jax.ShapeDtypeStruct((TOK, 2 * N), F32),
            jax.ShapeDtypeStruct((R, D), F32),
            jax.ShapeDtypeStruct((R, COLS), F32),
            jax.ShapeDtypeStruct((1, D, COLS), BF16),
        ),
        in_specs=[vm] * 6,
        out_specs=[hbm] * 4,
        scratch_shapes=[VMEM((D, COLS), BF16), dma((3,)), dma((D // ROWS,))],
        compiler_params=pltpu.CompilerParams(vmem_limit_bytes=16 * MIB),
        cost_estimate=pl.CostEstimate(flops=2 * D * COLS * 128, bytes_accessed=11_000_000, transcendentals=0),
    )(*(pltpu.with_memory_space_constraint(v, VMEM) for v in held))


def solution(mesh):
    in_specs = (
        P("dp", None),
        P("dp", "tensor"),
        P("dp", None),
        P("dp", None),
        P("dp", "tensor"),
        P("tensor"),
        P("dp", "tensor"),
        P(),
        P("dp", None, "tensor"),
    )
    out_specs = (P("dp", None), P("tensor", None), P(None, "tensor"), P("dp", None, "tensor"))
    return jax.shard_map(body, mesh=mesh, in_specs=in_specs, out_specs=out_specs, check_vma=False)
```

```python
import jax
import jax.numpy as jnp
from jax import lax
from jax.experimental import pallas as pl
from jax.experimental.pallas import tpu as pltpu
from jax.sharding import PartitionSpec as P

R = 32
TOK = 768
D = 1280
COLS = 1280
HEADS = 20
N = 128
BLK = 128
NB = TOK // BLK
PAIRS = HEADS // 2
NX, NY, NZ = 4, 4, 8
PLANE = NX * NY
PR, PC = 8, 384
WIDE = NY * PC
ROWS = 256
F32 = jnp.float32
BF16 = jnp.bfloat16
MESH = pl.DeviceIdType.MESH
VMEM = pltpu.VMEM
MIB = 1024 * 1024

NN = (((1,), (0,)), ((), ()))
NT = (((1,), (1,)), ((), ()))
TN = (((0,), (0,)), ((), ()))


def hops(k, size):
    return min(k, size - k)


IN_PLANE = sorted(range(1, PLANE), key=lambda k: -hops(k // NX, NY) - hops(k % NX, NX))
ON_LINE = sorted(range(1, NZ), key=lambda k: -hops(k, NZ))
NEAR_FIRST = sorted(range(NY), key=lambda k: hops(k, NY))


def mm(a, b, dims=NN):
    return lax.dot_general(a, b, dims, preferred_element_type=F32)


def narrow(a, b):
    a1, a2, a3 = split3(a)
    b1, b2, b3 = split3(b)
    zero = jnp.zeros((R, 2 * R), BF16)
    return mm(
        jnp.concatenate([a1, a1, a2, a1, a2, a3, zero], axis=1),
        jnp.concatenate([b1, b2, b1, b3, b2, b1, b1, b1], axis=0),
    )


def split2(v):
    hi = v.astype(BF16)
    lo = (v - hi.astype(F32)).astype(BF16)
    return hi, lo


def split3(v):
    hi = v.astype(BF16)
    rest = v - hi.astype(F32)
    mid = rest.astype(BF16)
    lo = (rest - mid.astype(F32)).astype(BF16)
    return hi, mid, lo


def stack3(v):
    return jnp.concatenate(split3(v), axis=0)


def fold3(v):
    return v[0:R] + v[R : 2 * R] + v[2 * R : 3 * R]


def iota(shape, dim):
    return lax.broadcasted_iota(jnp.int32, shape, dim)


def block(c):
    return pl.ds(pl.multiple_of(c * BLK, BLK), BLK)


def mod(a):
    quotient = (a.astype(F32) * (1.0 / 46337.0)).astype(jnp.int32)
    left = a - quotient * 46337
    left = jnp.where(left < 0, left + 46337, left)
    return jnp.where(left >= 46337, left - 46337, left)


def start_factor(seed, offset):
    rank = iota((R, COLS), 0)
    column = iota((R, COLS), 1) + offset
    one = mod(rank * 7919 + column * 104 + seed)
    two = mod(one * one)
    three = mod(two * 211 + column * 13 + rank)
    four = mod(three * three)
    return four.astype(F32) * (2.0 / 46337.0) - 1.0


def inverse_factor(gram):
    work = jnp.concatenate(
        [gram, (iota((R, R), 0) == iota((R, R), 1)).astype(F32), jnp.zeros((R, 128 - 2 * R), F32)], axis=1
    )
    row_at = iota((R, 128), 0)
    diag = jnp.ones((R, 128), F32)
    for k in range(R):
        column = jnp.broadcast_to(work[:, k : k + 1], (R, 128))
        pivot = column[k : k + 1, :]
        diag = jnp.where(row_at == k, pivot, diag)
        scaled = work[k : k + 1, :] / pivot
        work = work - jnp.where(row_at > k, column, 0.0) * scaled
    return (work * lax.rsqrt(diag))[:, R : 2 * R]


class Comm:
    def __init__(self, local, full, slots, line, sems):
        self.local, self.full, self.slots, self.line, self.sems = local, full, slots, line, sems
        at = lax.axis_index("dp")
        self.core = lax.axis_index("tensor")
        self.x = lax.rem(at, NX)
        self.z = lax.rem(at // NX, NZ)
        self.y = at // (NX * NZ)

    def device(self, y, z, x):
        return ((y * NZ + z) * NX + x, self.core)

    def neighbour(self, k):
        return lax.rem(self.y + k // NX, NY), lax.rem(self.x + k % NX, NX)

    def greet(self, barrier):
        for k in IN_PLANE:
            y, x = self.neighbour(k)
            pl.semaphore_signal(barrier, inc=1, device_id=self.device(y, self.z, x), device_id_type=MESH)
        for k in ON_LINE:
            z = lax.rem(self.z + k, NZ)
            pl.semaphore_signal(barrier, inc=1, device_id=self.device(self.y, z, self.x), device_id_type=MESH)

    def piece(self, ref, y, x):
        return ref.at[pl.ds(pl.multiple_of(x * PR, PR), PR), pl.ds(pl.multiple_of(y * PC, 128), PC)]

    def scatter(self, k):
        y, x = self.neighbour(k)
        return pltpu.make_async_remote_copy(
            src_ref=self.piece(self.local, y, x),
            dst_ref=self.slots.at[k],
            send_sem=self.sems.at[0, k],
            recv_sem=self.sems.at[1, k],
            device_id=self.device(y, self.z, x),
            device_id_type=MESH,
        )

    def along(self, k):
        return pltpu.make_async_remote_copy(
            src_ref=self.line.at[self.z],
            dst_ref=self.line.at[self.z],
            send_sem=self.sems.at[2, k],
            recv_sem=self.sems.at[3, k],
            device_id=self.device(self.y, lax.rem(self.z + k, NZ), self.x),
            device_id_type=MESH,
        )

    def gather(self, k):
        y, x = self.neighbour(k)
        mine = self.piece(self.full, self.y, self.x)
        return pltpu.make_async_remote_copy(
            src_ref=mine,
            dst_ref=mine,
            send_sem=self.sems.at[4, k],
            recv_sem=self.sems.at[5, k],
            device_id=self.device(y, self.z, x),
            device_id_type=MESH,
        )

    def begin(self):
        for k in IN_PLANE:
            self.scatter(k).start()

    def middle(self):
        total = self.piece(self.local, self.y, self.x)[...]
        for k in IN_PLANE[::-1]:
            self.scatter(k).wait_recv()
            total = total + self.slots[k]
        self.line[self.z] = total
        for k in ON_LINE:
            self.along(k).start()

    def last(self):
        for k in ON_LINE[::-1]:
            self.along(k).wait_recv()
        total = self.line[0]
        for k in range(1, NZ):
            total = total + self.line[k]
        self.piece(self.full, self.y, self.x)[...] = total
        for k in IN_PLANE:
            self.gather(k).start()

    def end_part(self, dy):
        for k in range(NX * dy, NX * dy + NX):
            if k:
                self.gather(k).wait_recv()
        return lax.rem(self.y + NY - dy, NY)

    def end(self):
        for dy in NEAR_FIRST:
            self.end_part(dy)

    def settle(self):
        for k in IN_PLANE:
            self.scatter(k).wait_send()
            self.gather(k).wait_send()
        for k in ON_LINE:
            self.along(k).wait_send()


def main_kernel(
    seed_ref, feat_hbm, x_hbm, b_hbm, c_hbm, ld_hbm, gain_hbm, dy_hbm, err_hbm,
    whole_hi, whole_lo, p_out, q_out, gbc_out, left_out, right_out,
    feat, xin, dy, err, b_in, c_in, ld_in, gain_in, gx,
    ldp, gainp, gain_row, grows, remain, decays, dys, after, after16, state, passing,
    start, first_part, gbc, other,
    local_p, full_p, slots_p, line_p, local_q, full_q, slots_q, line_q,
    sems_p, sems_q, pair_sems, in_sems, dy_sems, err_sems,
):
    first = Comm(local_p, full_p, slots_p, line_p, sems_p)
    second = Comm(local_q, full_q, slots_q, line_q, sems_q)
    core = first.core
    at = lax.axis_index("dp")

    def dy_copy(c):
        return pltpu.make_async_copy(dy_hbm.at[block(c), :], dy.at[block(c), :], dy_sems.at[c])

    def err_copy(i):
        rows = pl.ds(pl.multiple_of(i * ROWS, ROWS), ROWS)
        return pltpu.make_async_copy(err_hbm.at[rows, :], err.at[rows, :], err_sems.at[i])

    small = [(ld_hbm, ld_in), (b_hbm, b_in), (c_hbm, c_in), (gain_hbm, gain_in)]
    small = [pltpu.make_async_copy(s, d, in_sems.at[i]) for i, (s, d) in enumerate(small)]
    feat_copy = pltpu.make_async_copy(feat_hbm, feat, in_sems.at[4])
    x_copy = pltpu.make_async_copy(x_hbm, xin, in_sems.at[5])
    for copy in small:
        copy.start()
    dy_copy(NB - 1).start()

    barrier = pltpu.get_barrier_semaphore()
    first.greet(barrier)
    pl.semaphore_signal(barrier, inc=1, device_id=(at, 1 - core), device_id_type=MESH)

    local_p[:, D:] = jnp.zeros((R, WIDE - D), F32)
    local_q[:, D:] = jnp.zeros((R, WIDE - D), F32)
    whole_hi[D:, :] = jnp.zeros((WIDE - D, COLS), BF16)
    whole_lo[D:, :] = jnp.zeros((WIDE - D, COLS), BF16)
    ldp[...] = jnp.zeros((128, TOK), F32)
    gainp[...] = jnp.zeros((8, 128), F32)
    after[...] = jnp.zeros((N, COLS), F32)
    state[...] = jnp.zeros((N, COLS), F32)
    factor3 = stack3(start_factor(seed_ref[0], core * COLS))
    start[...] = jnp.concatenate([factor3, jnp.zeros((R, COLS), BF16)], axis=0).T
    expand = (iota((128, COLS), 0) == iota((128, COLS), 1) // 64).astype(BF16)
    expand2 = jnp.concatenate([expand, expand], axis=0)
    lower = (iota((BLK, BLK), 0) >= iota((BLK, BLK), 1)).astype(BF16)
    lower3 = jnp.concatenate([lower, lower, lower], axis=1)
    causal = iota((BLK, BLK), 0) <= iota((BLK, BLK), 1)
    low_half = iota((BLK, 128), 1) < 64

    for copy in small:
        copy.wait()
    for c in range(NB - 2, -1, -1):
        dy_copy(c).start()
    for i in range(D // ROWS):
        err_copy(i).start()
    feat_copy.start()
    x_copy.start()
    ldp[0:HEADS, :] = ld_in[...]
    gainp[0:1, 0:HEADS] = gain_in[...]
    gain_hi, gain_mid, gain_lo = split3(gainp[...])
    gain_row[...] = mm(gain_hi, expand) + mm(gain_mid, expand) + mm(gain_lo, expand)

    turns = [mm(jnp.concatenate(split3(ldp[:, block(c)]), axis=1), lower3, NT) for c in range(NB)]
    totals = [turned.T for turned in turns]
    begun = jnp.concatenate([jnp.exp(total) for total in totals], axis=0)
    begun = mm(jnp.concatenate(split2(begun), axis=1), expand2)
    grows[...] = begun
    for c in range(NB):
        passing[8 * c : 8 * c + 8, :] = begun[(c + 1) * BLK - 8 : (c + 1) * BLK]
    ended = jnp.concatenate([jnp.exp(total[BLK - 1 : BLK, :] - total) for total in totals], axis=0)
    remain[...] = mm(jnp.concatenate(split2(ended), axis=1), expand2)

    def masked(dy_pair):
        zero = jnp.zeros_like(dy_pair)
        return jnp.concatenate([jnp.where(low_half, dy_pair, zero), jnp.where(low_half, zero, dy_pair)], axis=0)

    def token_block(c, more):
        rows = block(c)
        total, turned = totals[c], turns[c]
        grow, left = grows[rows, :], remain[rows, :]
        dy_scaled, dy_rest = split2(dy[rows, :].astype(F32) * grow)
        dys[rows, :] = dy_scaled
        b_blk, c_blk = b_in[rows, :], c_in[rows, :]
        now = after[...]
        now16, now_rest = split2(now)
        after16[rows, :] = now16
        carried = mm(jnp.concatenate([b_blk, b_blk], axis=1), jnp.concatenate([now16, now_rest], axis=0)) * left
        scores = jnp.where(causal, mm(b_blk, c_blk, NT), 0.0)
        scores2 = jnp.concatenate([scores, scores], axis=1)
        for j in range(PAIRS):
            lanes = slice(128 * j, 128 * j + 128)
            dy_pair = dy[rows, lanes]
            both = masked(dy_pair)
            h = 2 * j
            to_row = jnp.concatenate([turned[h : h + 1, :], turned[h + 1 : h + 2, :]], axis=1)
            from_col = jnp.concatenate(
                [
                    jnp.broadcast_to(total[:, h : h + 1], (BLK, BLK)),
                    jnp.broadcast_to(total[:, h + 1 : h + 2], (BLK, BLK)),
                ],
                axis=1,
            )
            decay = jnp.exp(jnp.minimum(to_row - from_col, 0.0))
            decays[rows, 256 * j : 256 * j + 256] = decay
            weights, weights_rest = split2(decay * scores2)
            grad_x = mm(weights, both) + mm(weights_rest, both)
            grad_x = grad_x + gain_row[0:1, lanes] * dy_pair.astype(F32) + carried[:, lanes]
            gx[rows, lanes] = grad_x.astype(BF16)
        if more:
            after[...] = now * grow[BLK - 1 : BLK] + mm(
                jnp.concatenate([c_blk, c_blk], axis=0), jnp.concatenate([dy_scaled, dy_rest], axis=0), TN
            )

    def project(low, high):
        rows = slice(low * BLK, high * BLK)
        return fold3(mm(stack3(fold3(mm(gx[rows, :], start[...]).T)), feat[rows, :]))

    for c in range(NB - 1, -1, -1):
        if c >= NB - 2:
            dy_copy(c).wait()
        elif c == NB - 3:
            for k in range(NB - 3, -1, -1):
                dy_copy(k).wait()
            for i in range(D // ROWS):
                err_copy(i).wait()
        elif c == 0:
            feat_copy.wait()
            early = project(1, NB)
        token_block(c, c > 0)
        if NB - 3 >= c > 0:
            for i in range(2 * (NB - 3 - c), min(2 * (NB - 3 - c) + 2, D // ROWS)):
                rows = pl.ds(i * ROWS, ROWS)
                first_part[:, rows] = fold3(mm(err[rows, :], start[...]).T)
    local_p[:, :D] = first_part[...] + (early + project(0, 1)) * (1.0 / TOK)

    pl.semaphore_wait(barrier, PLANE - 1 + NZ - 1 + 1)
    first.begin()

    def whole_rows(i):
        rows = pl.ds(i * ROWS, ROWS)
        part = mm(feat[:, i * ROWS : (i + 1) * ROWS], gx[...], TN)
        whole_hi[rows, :], whole_lo[rows, :] = split2(part * (1.0 / TOK) + err[rows, :].astype(F32))

    def bc_block(c, carry):
        rows = block(c)
        b_blk, c_blk = b_in[rows, :], c_in[rows, :]
        x_scaled = (xin[rows, :].astype(F32) * remain[rows, :]).astype(BF16)
        before = state[...]
        grad_b = mm(x_scaled, after16[rows, :], NT)
        grad_c = mm(dys[rows, :], before.astype(BF16), NT)
        factor = passing[pl.ds(pl.multiple_of(8 * c, 8), 8), :][7:8, :]
        state[...] = before * factor + mm(b_blk, x_scaled, TN)
        gaps = jnp.zeros((BLK, BLK), F32)
        for j in range(PAIRS):
            lanes = slice(128 * j, 128 * j + 128)
            products = mm(xin[rows, lanes], masked(dy[rows, lanes]), NT) * decays[rows, 256 * j : 256 * j + 256]
            gaps = gaps + products[:, :BLK] + products[:, BLK:]
        gap_hi, gap_lo = split2(jnp.where(causal, gaps, 0.0))
        gbc[rows, 0:N] = grad_b + mm(gap_hi, c_blk) + mm(gap_lo, c_blk)
        gbc[rows, N : 2 * N] = grad_c + mm(gap_hi, b_blk, TN) + mm(gap_lo, b_blk, TN)
        return carry

    for i in range(D // ROWS):
        whole_rows(i)
    first.middle()
    x_copy.wait()
    lax.fori_loop(0, NB // 2, bc_block, 0)
    first.last()
    lax.fori_loop(NB // 2, NB, bc_block, 0)
    swap = pltpu.make_async_remote_copy(
        src_ref=gbc,
        dst_ref=other,
        send_sem=pair_sems.at[0],
        recv_sem=pair_sems.at[1],
        device_id=(at, 1 - core),
        device_id_type=MESH,
    )
    swap.start()

    own = jnp.zeros((3 * R, COLS), F32)
    for dy_hops in NEAR_FIRST:
        columns = pl.ds(pl.multiple_of(first.end_part(dy_hops) * PC, 128), PC)
        part = stack3(full_p[:, columns])
        own = own + mm(part, whole_hi[columns, :]) + mm(part, whole_lo[columns, :])
    local_q[:, :COLS] = fold3(own)
    second.begin()

    psum = full_p[:, :D]
    parts = stack3(psum)
    cross = mm(parts, parts, NT)
    gram = jnp.zeros((R, R), F32)
    for a in range(2, -1, -1):
        for b in range(2, -1, -1):
            gram = gram + cross[R * a : R * a + R, R * b : R * b + R]
    inverse = inverse_factor(gram)
    second.middle()

    basis = narrow(inverse, psum)
    p_out[...] = basis
    p_hi, p_lo = split2(basis * (1.0 / 128.0))
    left_out[...] = jnp.concatenate([p_hi, p_hi, p_lo, p_lo], axis=0).T
    second.last()

    swap.wait()
    gbc_out[...] = gbc[...] + other[...]
    first.settle()
    second.end()

    summed = narrow(inverse, full_q[:, :COLS])
    q_out[...] = summed
    q_hi, q_lo = split2(summed)
    right_out[...] = jnp.concatenate([q_hi, q_lo, q_hi, q_lo], axis=0)
    second.settle()


def last_kernel(whole_hi, whole_lo, p_in, q_in, gbc_in, left, right, gbc_out, p_out, q_out, err_out, done, sems, out_sems):
    copies = [
        pltpu.make_async_copy(gbc_in, gbc_out, sems.at[0]),
        pltpu.make_async_copy(p_in, p_out, sems.at[1]),
        pltpu.make_async_copy(q_in, q_out, sems.at[2]),
    ]
    for copy in copies:
        copy.start()
    for i in range(D // ROWS):
        rows = pl.ds(i * ROWS, ROWS)
        whole = whole_hi[rows, :].astype(F32) + whole_lo[rows, :].astype(F32)
        done[rows, :] = (whole - mm(left[rows, :], right[...])).astype(BF16)
        copy = pltpu.make_async_copy(done.at[rows, :], err_out.at[0, rows, :], out_sems.at[i])
        copy.start()
        copies.append(copy)
    for copy in copies:
        copy.wait()


def body(layer_in, ssm_in, b_in, c_in, log_decay, skip_gain, grad_out, q_seed, error_in):
    vm = pl.BlockSpec(memory_space=VMEM)
    hbm = pl.BlockSpec(memory_space=pltpu.HBM)
    piece = VMEM((R, WIDE), F32)
    slots = VMEM((PLANE, PR, PC), F32)
    line = VMEM((NZ, PR, PC), F32)
    tokens16 = VMEM((TOK, COLS), BF16)
    tokens32 = VMEM((TOK, COLS), F32)
    dma = pltpu.SemaphoreType.DMA
    held = pl.pallas_call(
        main_kernel,
        out_shape=(
            VMEM((WIDE, COLS), BF16),
            VMEM((WIDE, COLS), BF16),
            VMEM((R, D), F32),
            VMEM((R, COLS), F32),
            VMEM((TOK, 2 * N), F32),
            VMEM((D, 4 * R), BF16),
            VMEM((4 * R, COLS), BF16),
        ),
        in_specs=[pl.BlockSpec(memory_space=pltpu.SMEM)] + [hbm] * 8,
        out_specs=[vm] * 7,
        scratch_shapes=[
            tokens16, tokens16, tokens16,
            VMEM((D, COLS), BF16),
            VMEM((TOK, N), BF16), VMEM((TOK, N), BF16),
            VMEM((HEADS, TOK), F32), VMEM((1, HEADS), F32),
            tokens16,
            VMEM((128, TOK), F32),
            VMEM((8, 128), F32), VMEM((8, COLS), F32),
            tokens32, tokens32,
            VMEM((TOK, HEADS * BLK), F32),
            tokens16,
            VMEM((N, COLS), F32),
            tokens16,
            VMEM((N, COLS), F32),
            VMEM((8 * NB, COLS), F32),
            VMEM((COLS, 4 * R), BF16),
            VMEM((R, D), F32),
            VMEM((TOK, 2 * N), F32), VMEM((TOK, 2 * N), F32),
            piece, piece, slots, line,
            piece, piece, slots, line,
            dma((6, PLANE)), dma((6, PLANE)), dma((2,)), dma((6,)), dma((NB,)), dma((D // ROWS,)),
        ],
        compiler_params=pltpu.CompilerParams(
            collective_id=0, has_side_effects=True, vmem_limit_bytes=48 * MIB
        ),
        cost_estimate=pl.CostEstimate(
            flops=2 * D * COLS * 2200, bytes_accessed=20_000_000, transcendentals=TOK * BLK * HEADS
        ),
    )(
        q_seed,
        *(
            pltpu.with_memory_space_constraint(v, pltpu.HBM)
            for v in (
                layer_in, ssm_in, b_in, c_in, log_decay.T, skip_gain.reshape(1, HEADS), grad_out,
                error_in.reshape(D, COLS),
            )
        ),
    )
    return pl.pallas_call(
        last_kernel,
        out_shape=(
            jax.ShapeDtypeStruct((TOK, 2 * N), F32),
            jax.ShapeDtypeStruct((R, D), F32),
            jax.ShapeDtypeStruct((R, COLS), F32),
            jax.ShapeDtypeStruct((1, D, COLS), BF16),
        ),
        in_specs=[vm] * 7,
        out_specs=[hbm] * 4,
        scratch_shapes=[VMEM((D, COLS), BF16), dma((3,)), dma((D // ROWS,))],
        compiler_params=pltpu.CompilerParams(vmem_limit_bytes=16 * MIB),
        cost_estimate=pl.CostEstimate(flops=2 * D * COLS * 128, bytes_accessed=11_000_000, transcendentals=0),
    )(*(pltpu.with_memory_space_constraint(v, VMEM) for v in held))


def solution(mesh):
    in_specs = (
        P("dp", None),
        P("dp", "tensor"),
        P("dp", None),
        P("dp", None),
        P("dp", "tensor"),
        P("tensor"),
        P("dp", "tensor"),
        P(),
        P("dp", None, "tensor"),
    )
    out_specs = (P("dp", None), P("tensor", None), P(None, "tensor"), P("dp", None, "tensor"))
    return jax.shard_map(body, mesh=mesh, in_specs=in_specs, out_specs=out_specs, check_vma=False)
```

```python
import jax
import jax.numpy as jnp
from jax import lax
from jax.experimental import pallas as pl
from jax.experimental.pallas import tpu as pltpu
from jax.sharding import PartitionSpec as P

R = 32
TOK = 768
D = 1280
COLS = 1280
HEADS = 20
N = 128
BLK = 128
NB = TOK // BLK
PAIRS = HEADS // 2
NX, NY, NZ = 4, 4, 8
PLANE = NX * NY
PR, PC = 8, 384
WIDE = NY * PC
ROWS = 256
F32 = jnp.float32
BF16 = jnp.bfloat16
MESH = pl.DeviceIdType.MESH
VMEM = pltpu.VMEM
MIB = 1024 * 1024

NN = (((1,), (0,)), ((), ()))
NT = (((1,), (1,)), ((), ()))
TN = (((0,), (0,)), ((), ()))


def hops(k, size):
    return min(k, size - k)


IN_PLANE = sorted(range(1, PLANE), key=lambda k: -hops(k // NX, NY) - hops(k % NX, NX))
ON_LINE = sorted(range(1, NZ), key=lambda k: -hops(k, NZ))
NEAR_FIRST = sorted(range(NY), key=lambda k: hops(k, NY))


def mm(a, b, dims=NN):
    return lax.dot_general(a, b, dims, preferred_element_type=F32)


def narrow(a, b):
    a1, a2, a3 = split3(a)
    b1, b2, b3 = split3(b)
    zero = jnp.zeros((R, 2 * R), BF16)
    return mm(
        jnp.concatenate([a1, a1, a2, a1, a2, a3, zero], axis=1),
        jnp.concatenate([b1, b2, b1, b3, b2, b1, b1, b1], axis=0),
    )


def split2(v):
    hi = v.astype(BF16)
    lo = (v - hi.astype(F32)).astype(BF16)
    return hi, lo


def split3(v):
    hi = v.astype(BF16)
    rest = v - hi.astype(F32)
    mid = rest.astype(BF16)
    lo = (rest - mid.astype(F32)).astype(BF16)
    return hi, mid, lo


def stack3(v):
    return jnp.concatenate(split3(v), axis=0)


def fold3(v):
    return v[0:R] + v[R : 2 * R] + v[2 * R : 3 * R]


def iota(shape, dim):
    return lax.broadcasted_iota(jnp.int32, shape, dim)


def block(c):
    return pl.ds(pl.multiple_of(c * BLK, BLK), BLK)


def mod(a):
    quotient = (a.astype(F32) * (1.0 / 46337.0)).astype(jnp.int32)
    left = a - quotient * 46337
    left = jnp.where(left < 0, left + 46337, left)
    return jnp.where(left >= 46337, left - 46337, left)


def start_factor(seed, offset):
    rank = iota((R, COLS), 0)
    column = iota((R, COLS), 1) + offset
    one = mod(rank * 7919 + column * 104 + seed)
    two = mod(one * one)
    three = mod(two * 211 + column * 13 + rank)
    four = mod(three * three)
    return four.astype(F32) * (2.0 / 46337.0) - 1.0


def inverse_factor(gram):
    work = jnp.concatenate(
        [gram, (iota((R, R), 0) == iota((R, R), 1)).astype(F32), jnp.zeros((R, 128 - 2 * R), F32)], axis=1
    )
    row_at = iota((R, 128), 0)
    diag = jnp.ones((R, 128), F32)
    for k in range(R):
        column = jnp.broadcast_to(work[:, k : k + 1], (R, 128))
        pivot = column[k : k + 1, :]
        diag = jnp.where(row_at == k, pivot, diag)
        scaled = work[k : k + 1, :] / pivot
        work = work - jnp.where(row_at > k, column, 0.0) * scaled
    return (work * lax.rsqrt(diag))[:, R : 2 * R]


class Comm:
    def __init__(self, local, full, slots, line, sems):
        self.local, self.full, self.slots, self.line, self.sems = local, full, slots, line, sems
        at = lax.axis_index("dp")
        self.core = lax.axis_index("tensor")
        self.x = lax.rem(at, NX)
        self.z = lax.rem(at // NX, NZ)
        self.y = at // (NX * NZ)

    def device(self, y, z, x):
        return ((y * NZ + z) * NX + x, self.core)

    def neighbour(self, k):
        return lax.rem(self.y + k // NX, NY), lax.rem(self.x + k % NX, NX)

    def greet(self, barrier):
        for k in IN_PLANE:
            y, x = self.neighbour(k)
            pl.semaphore_signal(barrier, inc=1, device_id=self.device(y, self.z, x), device_id_type=MESH)
        for k in ON_LINE:
            z = lax.rem(self.z + k, NZ)
            pl.semaphore_signal(barrier, inc=1, device_id=self.device(self.y, z, self.x), device_id_type=MESH)

    def piece(self, ref, y, x):
        return ref.at[pl.ds(pl.multiple_of(x * PR, PR), PR), pl.ds(pl.multiple_of(y * PC, 128), PC)]

    def scatter(self, k):
        y, x = self.neighbour(k)
        return pltpu.make_async_remote_copy(
            src_ref=self.piece(self.local, y, x),
            dst_ref=self.slots.at[k],
            send_sem=self.sems.at[0, k],
            recv_sem=self.sems.at[1, k],
            device_id=self.device(y, self.z, x),
            device_id_type=MESH,
        )

    def along(self, k):
        return pltpu.make_async_remote_copy(
            src_ref=self.line.at[self.z],
            dst_ref=self.line.at[self.z],
            send_sem=self.sems.at[2, k],
            recv_sem=self.sems.at[3, k],
            device_id=self.device(self.y, lax.rem(self.z + k, NZ), self.x),
            device_id_type=MESH,
        )

    def gather(self, k):
        y, x = self.neighbour(k)
        mine = self.piece(self.full, self.y, self.x)
        return pltpu.make_async_remote_copy(
            src_ref=mine,
            dst_ref=mine,
            send_sem=self.sems.at[4, k],
            recv_sem=self.sems.at[5, k],
            device_id=self.device(y, self.z, x),
            device_id_type=MESH,
        )

    def begin(self):
        for k in IN_PLANE:
            self.scatter(k).start()

    def middle(self):
        total = self.piece(self.local, self.y, self.x)[...]
        for k in IN_PLANE[::-1]:
            self.scatter(k).wait_recv()
            total = total + self.slots[k]
        self.line[self.z] = total
        for k in ON_LINE:
            self.along(k).start()

    def last(self):
        for k in ON_LINE[::-1]:
            self.along(k).wait_recv()
        total = self.line[0]
        for k in range(1, NZ):
            total = total + self.line[k]
        self.piece(self.full, self.y, self.x)[...] = total
        for k in IN_PLANE:
            self.gather(k).start()

    def end_part(self, dy):
        for k in range(NX * dy, NX * dy + NX):
            if k:
                self.gather(k).wait_recv()
        return lax.rem(self.y + NY - dy, NY)

    def end(self):
        for dy in NEAR_FIRST:
            self.end_part(dy)

    def settle(self):
        for k in IN_PLANE:
            self.scatter(k).wait_send()
            self.gather(k).wait_send()
        for k in ON_LINE:
            self.along(k).wait_send()


def main_kernel(
    seed_ref, feat_hbm, x_hbm, b_hbm, c_hbm, ld_hbm, gain_hbm, dy_hbm, err_hbm,
    whole_hi, whole_lo, p_out, q_out, gbc_out, left_out, right_out,
    feat, xin, dy, err, b_in, c_in, ld_in, gain_in, gx,
    ldp, gainp, gain_row, grows, remain, decays, dys, after, after16, state, passing,
    start, first_part, gbc, other,
    local_p, full_p, slots_p, line_p, local_q, full_q, slots_q, line_q,
    sems_p, sems_q, pair_sems, in_sems, dy_sems, err_sems,
):
    first = Comm(local_p, full_p, slots_p, line_p, sems_p)
    second = Comm(local_q, full_q, slots_q, line_q, sems_q)
    core = first.core
    at = lax.axis_index("dp")

    def dy_copy(c):
        return pltpu.make_async_copy(dy_hbm.at[block(c), :], dy.at[block(c), :], dy_sems.at[c])

    def err_copy(i):
        rows = pl.ds(pl.multiple_of(i * ROWS, ROWS), ROWS)
        return pltpu.make_async_copy(err_hbm.at[rows, :], err.at[rows, :], err_sems.at[i])

    small = [(ld_hbm, ld_in), (b_hbm, b_in), (c_hbm, c_in), (gain_hbm, gain_in)]
    small = [pltpu.make_async_copy(s, d, in_sems.at[i]) for i, (s, d) in enumerate(small)]
    feat_copy = pltpu.make_async_copy(feat_hbm, feat, in_sems.at[4])
    x_copy = pltpu.make_async_copy(x_hbm, xin, in_sems.at[5])
    for copy in small:
        copy.start()
    dy_copy(NB - 1).start()

    barrier = pltpu.get_barrier_semaphore()
    first.greet(barrier)
    pl.semaphore_signal(barrier, inc=1, device_id=(at, 1 - core), device_id_type=MESH)

    local_p[:, D:] = jnp.zeros((R, WIDE - D), F32)
    local_q[:, D:] = jnp.zeros((R, WIDE - D), F32)
    whole_hi[D:, :] = jnp.zeros((WIDE - D, COLS), BF16)
    whole_lo[D:, :] = jnp.zeros((WIDE - D, COLS), BF16)
    ldp[...] = jnp.zeros((128, TOK), F32)
    gainp[...] = jnp.zeros((8, 128), F32)
    after[...] = jnp.zeros((N, COLS), F32)
    state[...] = jnp.zeros((N, COLS), F32)
    factor3 = stack3(start_factor(seed_ref[0], core * COLS))
    start[...] = jnp.concatenate([factor3, jnp.zeros((R, COLS), BF16)], axis=0).T
    expand = (iota((128, COLS), 0) == iota((128, COLS), 1) // 64).astype(BF16)
    expand2 = jnp.concatenate([expand, expand], axis=0)
    lower = (iota((BLK, BLK), 0) >= iota((BLK, BLK), 1)).astype(BF16)
    lower3 = jnp.concatenate([lower, lower, lower], axis=1)
    causal = iota((BLK, BLK), 0) <= iota((BLK, BLK), 1)
    low_half = iota((BLK, 128), 1) < 64

    small[0].wait()
    small[3].wait()
    for c in range(NB - 2, -1, -1):
        dy_copy(c).start()
    for i in range(D // ROWS):
        err_copy(i).start()
    feat_copy.start()
    x_copy.start()
    ldp[0:HEADS, :] = ld_in[...]
    gainp[0:1, 0:HEADS] = gain_in[...]
    gain_hi, gain_mid, gain_lo = split3(gainp[...])
    gain_row[...] = mm(gain_hi, expand) + mm(gain_mid, expand) + mm(gain_lo, expand)

    turns = [mm(jnp.concatenate(split3(ldp[:, block(c)]), axis=1), lower3, NT) for c in range(NB)]
    totals = [turned.T for turned in turns]
    begun = jnp.concatenate([jnp.exp(total) for total in totals], axis=0)
    begun = mm(jnp.concatenate(split2(begun), axis=1), expand2)
    grows[...] = begun
    for c in range(NB):
        passing[8 * c : 8 * c + 8, :] = begun[(c + 1) * BLK - 8 : (c + 1) * BLK]
    ended = jnp.concatenate([jnp.exp(total[BLK - 1 : BLK, :] - total) for total in totals], axis=0)
    remain[...] = mm(jnp.concatenate(split2(ended), axis=1), expand2)

    def masked(dy_pair):
        zero = jnp.zeros_like(dy_pair)
        return jnp.concatenate([jnp.where(low_half, dy_pair, zero), jnp.where(low_half, zero, dy_pair)], axis=0)

    def token_block(c, more):
        rows = block(c)
        total, turned = totals[c], turns[c]
        grow, left = grows[rows, :], remain[rows, :]
        dy_scaled, dy_rest = split2(dy[rows, :].astype(F32) * grow)
        dys[rows, :] = dy_scaled
        b_blk, c_blk = b_in[rows, :], c_in[rows, :]
        now = after[...]
        now16, now_rest = split2(now)
        after16[rows, :] = now16
        carried = mm(jnp.concatenate([b_blk, b_blk], axis=1), jnp.concatenate([now16, now_rest], axis=0)) * left
        scores = jnp.where(causal, mm(b_blk, c_blk, NT), 0.0)
        scores2 = jnp.concatenate([scores, scores], axis=1)
        for j in range(PAIRS):
            lanes = slice(128 * j, 128 * j + 128)
            dy_pair = dy[rows, lanes]
            both = masked(dy_pair)
            h = 2 * j
            to_row = jnp.concatenate([turned[h : h + 1, :], turned[h + 1 : h + 2, :]], axis=1)
            from_col = jnp.concatenate(
                [
                    jnp.broadcast_to(total[:, h : h + 1], (BLK, BLK)),
                    jnp.broadcast_to(total[:, h + 1 : h + 2], (BLK, BLK)),
                ],
                axis=1,
            )
            decay = jnp.exp(jnp.minimum(to_row - from_col, 0.0))
            decays[rows, 256 * j : 256 * j + 256] = decay
            weights, weights_rest = split2(decay * scores2)
            grad_x = mm(weights, both) + mm(weights_rest, both)
            grad_x = grad_x + gain_row[0:1, lanes] * dy_pair.astype(F32) + carried[:, lanes]
            gx[rows, lanes] = grad_x.astype(BF16)
        if more:
            after[...] = now * grow[BLK - 1 : BLK] + mm(
                jnp.concatenate([c_blk, c_blk], axis=0), jnp.concatenate([dy_scaled, dy_rest], axis=0), TN
            )

    def project(low, high):
        rows = slice(low * BLK, high * BLK)
        return fold3(mm(stack3(fold3(mm(gx[rows, :], start[...]).T)), feat[rows, :]))

    small[1].wait()
    small[2].wait()
    for c in range(NB - 1, -1, -1):
        if c >= NB - 2:
            dy_copy(c).wait()
        elif c == NB - 3:
            for k in range(NB - 3, -1, -1):
                dy_copy(k).wait()
            for i in range(D // ROWS):
                err_copy(i).wait()
        elif c == 0:
            feat_copy.wait()
            early = project(1, NB)
        token_block(c, c > 0)
        if NB - 3 >= c > 0:
            for i in range(2 * (NB - 3 - c), min(2 * (NB - 3 - c) + 2, D // ROWS)):
                rows = pl.ds(i * ROWS, ROWS)
                first_part[:, rows] = fold3(mm(err[rows, :], start[...]).T)
    local_p[:, :D] = first_part[...] + (early + project(0, 1)) * (1.0 / TOK)

    pl.semaphore_wait(barrier, PLANE - 1 + NZ - 1 + 1)
    first.begin()

    def whole_rows(i):
        rows = pl.ds(i * ROWS, ROWS)
        part = mm(feat[:, i * ROWS : (i + 1) * ROWS], gx[...], TN)
        whole_hi[rows, :], whole_lo[rows, :] = split2(part * (1.0 / TOK) + err[rows, :].astype(F32))

    def bc_block(c, carry):
        rows = block(c)
        b_blk, c_blk = b_in[rows, :], c_in[rows, :]
        x_scaled = (xin[rows, :].astype(F32) * remain[rows, :]).astype(BF16)
        before = state[...]
        grad_b = mm(x_scaled, after16[rows, :], NT)
        grad_c = mm(dys[rows, :], before.astype(BF16), NT)
        factor = passing[pl.ds(pl.multiple_of(8 * c, 8), 8), :][7:8, :]
        state[...] = before * factor + mm(b_blk, x_scaled, TN)
        gaps = jnp.zeros((BLK, BLK), F32)
        for j in range(PAIRS):
            lanes = slice(128 * j, 128 * j + 128)
            products = mm(xin[rows, lanes], masked(dy[rows, lanes]), NT) * decays[rows, 256 * j : 256 * j + 256]
            gaps = gaps + products[:, :BLK] + products[:, BLK:]
        gap_hi, gap_lo = split2(jnp.where(causal, gaps, 0.0))
        gbc[rows, 0:N] = grad_b + mm(gap_hi, c_blk) + mm(gap_lo, c_blk)
        gbc[rows, N : 2 * N] = grad_c + mm(gap_hi, b_blk, TN) + mm(gap_lo, b_blk, TN)
        return carry

    for i in range(D // ROWS):
        whole_rows(i)
    first.middle()
    x_copy.wait()
    lax.fori_loop(0, NB // 2, bc_block, 0)
    first.last()
    lax.fori_loop(NB // 2, NB, bc_block, 0)
    swap = pltpu.make_async_remote_copy(
        src_ref=gbc,
        dst_ref=other,
        send_sem=pair_sems.at[0],
        recv_sem=pair_sems.at[1],
        device_id=(at, 1 - core),
        device_id_type=MESH,
    )
    swap.start()

    own = jnp.zeros((3 * R, COLS), F32)
    for dy_hops in NEAR_FIRST:
        columns = pl.ds(pl.multiple_of(first.end_part(dy_hops) * PC, 128), PC)
        part = stack3(full_p[:, columns])
        own = own + mm(part, whole_hi[columns, :]) + mm(part, whole_lo[columns, :])
    local_q[:, :COLS] = fold3(own)
    second.begin()

    psum = full_p[:, :D]
    parts = stack3(psum)
    cross = mm(parts, parts, NT)
    gram = jnp.zeros((R, R), F32)
    for a in range(2, -1, -1):
        for b in range(2, -1, -1):
            gram = gram + cross[R * a : R * a + R, R * b : R * b + R]
    inverse = inverse_factor(gram)
    second.middle()

    basis = narrow(inverse, psum)
    p_out[...] = basis
    p_hi, p_lo = split2(basis * (1.0 / 128.0))
    left_out[...] = jnp.concatenate([p_hi, p_hi, p_lo, p_lo], axis=0).T
    second.last()

    swap.wait()
    gbc_out[...] = gbc[...] + other[...]
    first.settle()
    second.settle()
    second.end()

    summed = narrow(inverse, full_q[:, :COLS])
    q_out[...] = summed
    q_hi, q_lo = split2(summed)
    right_out[...] = jnp.concatenate([q_hi, q_lo, q_hi, q_lo], axis=0)


def last_kernel(whole_hi, whole_lo, p_in, q_in, gbc_in, left, right, gbc_out, p_out, q_out, err_out, done, sems, out_sems):
    copies = [
        pltpu.make_async_copy(gbc_in, gbc_out, sems.at[0]),
        pltpu.make_async_copy(p_in, p_out, sems.at[1]),
        pltpu.make_async_copy(q_in, q_out, sems.at[2]),
    ]
    for copy in copies:
        copy.start()
    for i in range(D // ROWS):
        rows = pl.ds(i * ROWS, ROWS)
        whole = whole_hi[rows, :].astype(F32) + whole_lo[rows, :].astype(F32)
        done[rows, :] = (whole - mm(left[rows, :], right[...])).astype(BF16)
        copy = pltpu.make_async_copy(done.at[rows, :], err_out.at[0, rows, :], out_sems.at[i])
        copy.start()
        copies.append(copy)
    for copy in copies:
        copy.wait()


def body(layer_in, ssm_in, b_in, c_in, log_decay, skip_gain, grad_out, q_seed, error_in):
    vm = pl.BlockSpec(memory_space=VMEM)
    hbm = pl.BlockSpec(memory_space=pltpu.HBM)
    piece = VMEM((R, WIDE), F32)
    slots = VMEM((PLANE, PR, PC), F32)
    line = VMEM((NZ, PR, PC), F32)
    tokens16 = VMEM((TOK, COLS), BF16)
    tokens32 = VMEM((TOK, COLS), F32)
    dma = pltpu.SemaphoreType.DMA
    held = pl.pallas_call(
        main_kernel,
        out_shape=(
            VMEM((WIDE, COLS), BF16),
            VMEM((WIDE, COLS), BF16),
            VMEM((R, D), F32),
            VMEM((R, COLS), F32),
            VMEM((TOK, 2 * N), F32),
            VMEM((D, 4 * R), BF16),
            VMEM((4 * R, COLS), BF16),
        ),
        in_specs=[pl.BlockSpec(memory_space=pltpu.SMEM)] + [hbm] * 8,
        out_specs=[vm] * 7,
        scratch_shapes=[
            tokens16, tokens16, tokens16,
            VMEM((D, COLS), BF16),
            VMEM((TOK, N), BF16), VMEM((TOK, N), BF16),
            VMEM((HEADS, TOK), F32), VMEM((1, HEADS), F32),
            tokens16,
            VMEM((128, TOK), F32),
            VMEM((8, 128), F32), VMEM((8, COLS), F32),
            tokens32, tokens32,
            VMEM((TOK, HEADS * BLK), F32),
            tokens16,
            VMEM((N, COLS), F32),
            tokens16,
            VMEM((N, COLS), F32),
            VMEM((8 * NB, COLS), F32),
            VMEM((COLS, 4 * R), BF16),
            VMEM((R, D), F32),
            VMEM((TOK, 2 * N), F32), VMEM((TOK, 2 * N), F32),
            piece, piece, slots, line,
            piece, piece, slots, line,
            dma((6, PLANE)), dma((6, PLANE)), dma((2,)), dma((6,)), dma((NB,)), dma((D // ROWS,)),
        ],
        compiler_params=pltpu.CompilerParams(
            collective_id=0, has_side_effects=True, vmem_limit_bytes=48 * MIB
        ),
        cost_estimate=pl.CostEstimate(
            flops=2 * D * COLS * 2200, bytes_accessed=20_000_000, transcendentals=TOK * BLK * HEADS
        ),
    )(
        q_seed,
        *(
            pltpu.with_memory_space_constraint(v, pltpu.HBM)
            for v in (
                layer_in, ssm_in, b_in, c_in, log_decay.T, skip_gain.reshape(1, HEADS), grad_out,
                error_in.reshape(D, COLS),
            )
        ),
    )
    return pl.pallas_call(
        last_kernel,
        out_shape=(
            jax.ShapeDtypeStruct((TOK, 2 * N), F32),
            jax.ShapeDtypeStruct((R, D), F32),
            jax.ShapeDtypeStruct((R, COLS), F32),
            jax.ShapeDtypeStruct((1, D, COLS), BF16),
        ),
        in_specs=[vm] * 7,
        out_specs=[hbm] * 4,
        scratch_shapes=[VMEM((D, COLS), BF16), dma((3,)), dma((D // ROWS,))],
        compiler_params=pltpu.CompilerParams(vmem_limit_bytes=16 * MIB),
        cost_estimate=pl.CostEstimate(flops=2 * D * COLS * 128, bytes_accessed=11_000_000, transcendentals=0),
    )(*(pltpu.with_memory_space_constraint(v, VMEM) for v in held))


def solution(mesh):
    in_specs = (
        P("dp", None),
        P("dp", "tensor"),
        P("dp", None),
        P("dp", None),
        P("dp", "tensor"),
        P("tensor"),
        P("dp", "tensor"),
        P(),
        P("dp", None, "tensor"),
    )
    out_specs = (P("dp", None), P("tensor", None), P(None, "tensor"), P("dp", None, "tensor"))
    return jax.shard_map(body, mesh=mesh, in_specs=in_specs, out_specs=out_specs, check_vma=False)
```
